512 devices in a mesh: ctx: 64 (over y, x, z_lo), head: 8 (over z_hi, core).
Axes of the slice: x: 4, y: 4, z: 16 (z_hi: 4, z_lo: 4; z = z_hi * 4 + z_lo), core: 2. Of those that a mesh axis runs over, the one named last changes fastest.
Arguments:
- x_seq: bfloat16 [16384, 4096], P('ctx', 'head'), may hold values from -0.29882812 to 0.29882812
- grad_out: bfloat16 [16384, 4096], P('ctx', 'head'), may hold values from -0.75 to 0.75
- b_proj: bfloat16 [16384, 128], P('ctx'), may hold values from -0.1796875 to 0.1796875
- c_proj: bfloat16 [16384, 128], P('ctx'), may hold values from -0.1796875 to 0.1796875
- decay_rate: float32 [64, 16384], P('head', 'ctx'), may hold values from 0.4 to 1
Outputs:
- grad_x: bfloat16 [16384, 4096], P('ctx', 'head')
- grad_b: float32 [16384, 128], P(('ctx', 'head'))
- grad_c: float32 [16384, 128], P(('ctx', 'head'))
The draws below stay inside these ranges and needn't reach their ends.
All inputs are finite; a program needn't handle non-finite values.
Results may differ from the reference program's by a relative error of at most 0.0061.
Values sent between devices are 32-bit elements; how exact they have to be, the bound alone decides.
A program may use at most 128 MiB of HBM per device.

```python
import math
import jax
import jax.numpy as jnp
from jax import lax

P_SIZE = 64
N = 128
Q = 256
TOK_DEV = 256
HEADS = 64
TOKEN_COUNT = 16384


def draw_decay_rate(key, part):
    key = jax.random.fold_in(key, 11)
    random_key_list = jax.random.split(key, 7)
    fast_share = 0.4
    slow_top = 1.0
    fast_heads = jax.random.uniform(random_key_list[0], (HEADS, 1)) < fast_share
    slow_total = jnp.exp(jax.random.uniform(random_key_list[1], (HEADS, 1), minval=math.log(0.05), maxval=math.log(slow_top)))
    fast_rate = jax.random.uniform(random_key_list[2], (HEADS, 1), minval=1.0 / 50.0, maxval=1.0 / 30.0)
    rate_base = jnp.where(fast_heads, fast_rate, slow_total / TOKEN_COUNT)
    devices = TOKEN_COUNT // TOK_DEV
    device_factor = jnp.exp(jax.random.uniform(random_key_list[3], (HEADS, devices), minval=math.log(0.5), maxval=math.log(2.0)))
    device_factor = jnp.repeat(device_factor, TOK_DEV, axis=1)
    roughness = jax.random.uniform(random_key_list[4], (HEADS, TOKEN_COUNT), minval=0.5, maxval=1.5)
    decay_factors = jnp.exp(-rate_base * device_factor * roughness)
    segment_location = jax.random.randint(random_key_list[5], (3,), 0, TOKEN_COUNT)
    segment_depth = jax.random.uniform(random_key_list[6], (3,), minval=0.5, maxval=0.8)
    causal_mask = jnp.arange(TOKEN_COUNT)[None, :] == segment_location[:, None]
    segment_factor = jnp.prod(jnp.where(causal_mask, segment_depth[:, None], 1.0), axis=0)
    return (decay_factors * segment_factor[None, :]).astype(jnp.float32)


def level_of(own_key, extent, pieces, least, largest):
    factor_of, own = 1.0, jax.random.fold_in(own_key, 6)
    for axis_at, parts in pieces:
        steps = jnp.exp(jax.random.uniform(jax.random.fold_in(own, axis_at), (parts,), jnp.float32, least / len(pieces), largest / len(pieces)))
        factor_of = factor_of * jnp.repeat(steps, extent[axis_at] // parts).reshape([-1 if axis == axis_at else 1 for axis in range(len(extent))])
    return factor_of


def bell_draw(stream_key, extent, deviation, limit, pieces=(), held_as=jnp.bfloat16):
    loudness = level_of(stream_key, extent, pieces, -0.22, 0.18) if pieces else 1.0
    values = jax.random.normal(stream_key, extent, jnp.float32) * deviation * loudness
    return jnp.minimum(jnp.maximum(values, -limit), limit).astype(held_as)


def setup_inputs(seed: int = 0) -> dict:
    streams_of = jax.random.split(jax.random.key(seed), 6)
    x_seq = bell_draw(streams_of[0], (TOKEN_COUNT, HEADS * P_SIZE), 0.05, 0.29882812, ((0, 64), (1, 8)))
    grad_out = bell_draw(streams_of[1], (TOKEN_COUNT, HEADS * P_SIZE), 0.125, 0.75, ((0, 64), (1, 8)))
    b_proj = bell_draw(streams_of[2], (TOKEN_COUNT, N), 0.03, 0.1796875, ((0, 64),))
    c_proj = bell_draw(streams_of[3], (TOKEN_COUNT, N), 0.03, 0.1796875, ((0, 64),))
    decay_rate = draw_decay_rate(jax.random.fold_in(streams_of[5], 71), 0)
    return dict(x_seq=x_seq, grad_out=grad_out, b_proj=b_proj, c_proj=c_proj, decay_rate=decay_rate)


def rounded(value):
    return lax.optimization_barrier(value.astype(jnp.bfloat16)).astype(jnp.float32)


def block_weights(cum_block):
    length = cum_block.shape[1]
    later_mask = lax.broadcasted_iota(jnp.int32, (length, length), 0) >= lax.broadcasted_iota(jnp.int32, (length, length), 1)
    spread = cum_block[:, :, None] - cum_block[:, None, :]
    return jnp.where(later_mask[None], jnp.exp(jnp.where(later_mask[None], spread, 0.0)), 0.0)


def scaled_rows(cum_block, b_float, c_float):
    to_end = jnp.exp(cum_block[:, -1:] - cum_block)
    from_start = jnp.exp(cum_block)
    b_scaled = rounded(b_float[None] * to_end[:, :, None])
    c_scaled = rounded(c_float[None] * from_start[:, :, None])
    return to_end, from_start, b_scaled, c_scaled


def reference(x_seq, grad_out, b_proj, c_proj, decay_rate):
    head_count = decay_rate.shape[0]
    tokens = x_seq.shape[0]
    blocks = tokens // Q
    head_width = x_seq.shape[1] // head_count
    state_size = b_proj.shape[1]
    cum_log = jnp.cumsum(jnp.log(decay_rate).reshape(head_count, blocks, Q), axis=2)
    cum_log = jnp.transpose(cum_log, (1, 0, 2))
    x_blocks = x_seq.reshape(blocks, Q, head_count, head_width)
    dy_blocks = grad_out.reshape(blocks, Q, head_count, head_width)
    b_blocks = b_proj.reshape(blocks, Q, state_size)
    c_blocks = c_proj.reshape(blocks, Q, state_size)
    inputs = (x_blocks, dy_blocks, b_blocks, c_blocks, cum_log)

    def forward_step(entering, block_args):
        x_blk, dy_blk, b_blk, c_blk, cum_block = block_args
        x_float = x_blk.astype(jnp.float32)
        dy_float = dy_blk.astype(jnp.float32)
        to_end, from_start, b_scaled, c_scaled = scaled_rows(cum_block, b_blk.astype(jnp.float32), c_blk.astype(jnp.float32))
        enter_b = rounded(entering)
        carried_c = jnp.sum(jnp.einsum('thp,hnp->htn', dy_float, enter_b) * from_start[:, :, None], axis=0)
        local_fwd = jnp.einsum('hsn,shp->hnp', b_scaled, x_float)
        block_gain = jnp.exp(cum_block[:, -1])
        return block_gain[:, None, None] * entering + local_fwd, carried_c

    def backward_step(leaving, block_args):
        x_blk, dy_blk, b_blk, c_blk, cum_block = block_args
        x_float = x_blk.astype(jnp.float32)
        dy_float = dy_blk.astype(jnp.float32)
        b_float = b_blk.astype(jnp.float32)
        c_float = c_blk.astype(jnp.float32)
        to_end, from_start, b_scaled, c_scaled = scaled_rows(cum_block, b_float, c_float)
        weights = block_weights(cum_block)
        inner_prod = jnp.einsum('tn,sn->ts', c_float, b_float)
        scores = rounded(inner_prod[None] * weights)
        pair_weights = rounded(jnp.einsum('thp,shp->hts', dy_float, x_float) * weights)
        leave_b = rounded(leaving)
        grad_x = jnp.einsum('hts,thp->shp', scores, dy_float) + jnp.einsum('hsn,hnp->shp', b_scaled, leave_b)
        grad_c = jnp.einsum('hts,sn->tn', pair_weights, b_float)
        grad_b = jnp.einsum('hts,tn->sn', pair_weights, c_float)
        grad_b = grad_b + jnp.sum(jnp.einsum('shp,hnp->hsn', x_float, leave_b) * to_end[:, :, None], axis=0)
        local_bwd = jnp.einsum('htn,thp->hnp', c_scaled, dy_float)
        block_gain = jnp.exp(cum_block[:, -1])
        next_state = local_bwd + block_gain[:, None, None] * leaving
        return next_state, (grad_x.astype(jnp.bfloat16), grad_b, grad_c)

    start_state = jnp.zeros((head_count, state_size, head_width), jnp.float32)
    ignored_fwd, carried_c = lax.scan(forward_step, start_state, inputs)
    ignored_bwd, outputs = lax.scan(backward_step, start_state, inputs, reverse=True)
    block_x, block_b, block_c = outputs
    grad_x = block_x.reshape(tokens, head_count * head_width)
    grad_b = block_b.reshape(tokens, state_size)
    grad_c = (block_c + carried_c).reshape(tokens, state_size)
    return grad_x, grad_b, grad_c
```

```python
import jax
import jax.numpy as jnp
from jax import lax
from jax.experimental import pallas as pl
from jax.experimental.pallas import tpu as pltpu
from jax.sharding import PartitionSpec as P

MESH = pl.DeviceIdType.MESH
Q = 256
HEADS = 8
WIDTH = 64
STATE = 128
BLOCKS = 4
GROUP = 32
ROWS = 16
LINES = 16
PART = 32

NN = (((1,), (0,)), ((), ()))
NT = (((1,), (1,)), ((), ()))
TN = (((0,), (0,)), ((), ()))


def dot(a, b, dims):
    return lax.dot_general(a, b, dims, preferred_element_type=jnp.float32)


def kernel(
    x_ref, dy_ref, b_ref, c_ref, decay_ref,
    gx_ref, gb_ref, gc_ref,
    fwd_out, bwd_out, gain_out, fwd_in, bwd_in, gain_in,
    fwd_tot, bwd_tot, gain_tot, fwd_oth, bwd_oth, gain_oth,
    enter_out, leave_out, enter_in, leave_in,
    xs_ref, ys_ref, end_ref, local_x, local_b, local_c,
    core_out, core_in, part_out, part_in,
    send_sems, recv_sems,
):
    me = lax.axis_index("ctx")
    head = lax.axis_index("head")
    line = me // 4
    half = (me // 2) % 2
    mine = line * 2 + me % 2
    core = head % 2
    z_hi = head // 2

    def ctx_of(i):
        return (i // 2) * 4 + half * 2 + i % 2

    other_half = {"ctx": line * 4 + (1 - half) * 2 + me % 2}
    other_core = {"head": z_hi * 2 + 1 - core}

    barrier = pltpu.get_barrier_semaphore()

    def greet(k, carry):
        pl.semaphore_signal(
            barrier, inc=1, device_id={"ctx": ctx_of(lax.rem(mine + k, GROUP))}, device_id_type=MESH
        )
        return carry

    lax.fori_loop(1, GROUP, greet, 0)
    pl.semaphore_signal(barrier, inc=1, device_id=other_half, device_id_type=MESH)
    pl.semaphore_signal(barrier, inc=1, device_id=other_core, device_id_type=MESH)
    for k in range(1, 4):
        pl.semaphore_signal(
            barrier, inc=1, device_id={"head": lax.rem(head + 2 * k, 8)}, device_id_type=MESH
        )

    lane = lax.broadcasted_iota(jnp.int32, (HEADS, Q), 1)
    cum = jnp.log(decay_ref[...])
    step = 1
    while step < Q:
        cum = cum + jnp.where(lane >= step, pltpu.roll(cum, step, 1), 0.0)
        step *= 2
    to_end = jnp.exp(cum[:, Q - 1 : Q] - cum)
    from_start = jnp.exp(cum)
    columns = jnp.transpose(jnp.concatenate([cum, to_end, from_start], axis=0))
    first_lanes = lax.broadcasted_iota(jnp.int32, (Q, 128), 1) < WIDTH
    b_blk = b_ref[...]
    c_blk = c_ref[...]

    def spread(base, block):
        left = jnp.broadcast_to(columns[:, base + 2 * block : base + 2 * block + 1], (Q, 128))
        right = jnp.broadcast_to(columns[:, base + 2 * block + 1 : base + 2 * block + 2], (Q, 128))
        return jnp.where(first_lanes, left, right)

    for block in range(BLOCKS):
        at = slice(block * 128, block * 128 + 128)
        end_blk = spread(HEADS, block)
        start_blk = spread(2 * HEADS, block)
        end_ref[:, at] = end_blk
        xs = (x_ref[:, at].astype(jnp.float32) * end_blk).astype(jnp.bfloat16)
        ys = (dy_ref[:, at].astype(jnp.float32) * start_blk).astype(jnp.bfloat16)
        xs_ref[:, at] = xs
        ys_ref[:, at] = ys
        gain_out[block] = start_blk[Q - 1 : Q, :]
        bwd_out[block * 8 : block * 8 + 8] = dot(c_blk, ys, TN).reshape(8, ROWS, 128)
        fwd_out[block * 8 : block * 8 + 8] = dot(b_blk, xs, TN).reshape(8, ROWS, 128)

    pl.semaphore_wait(barrier, GROUP - 1 + 1 + 1 + 3)

    def scatter(out, into, n):
        def one(k, carry):
            i = lax.rem(mine + k, GROUP)
            pltpu.make_async_remote_copy(
                src_ref=out.at[i], dst_ref=into.at[mine], send_sem=send_sems.at[n],
                recv_sem=recv_sems.at[n], device_id={"ctx": ctx_of(i)}, device_id_type=MESH,
            ).start()
            return carry

        lax.fori_loop(1, GROUP, one, 0)

    def send_gains(k, carry):
        i = lax.rem(mine + k, GROUP)
        pltpu.make_async_remote_copy(
            src_ref=gain_out.at[i // 8], dst_ref=gain_in.at[mine], send_sem=send_sems.at[0],
            recv_sem=recv_sems.at[0], device_id={"ctx": ctx_of(i)}, device_id_type=MESH,
        ).start()
        return carry

    def wait_bytes(ref, sems, n):
        pltpu.make_async_copy(ref, ref, sems.at[n]).wait()

    lax.fori_loop(1, GROUP, send_gains, 0)
    scatter(bwd_out, bwd_in, 1)
    scatter(fwd_out, fwd_in, 2)
    gain_in[mine] = gain_out[mine // 8]
    bwd_in[mine] = bwd_out[mine]
    fwd_in[mine] = fwd_out[mine]

    row = lax.broadcasted_iota(jnp.int32, (Q, Q), 0)
    col = lax.broadcasted_iota(jnp.int32, (Q, Q), 1)
    later = col >= row
    inner = dot(b_blk, c_blk, NT)
    pairs = jnp.zeros((Q, Q), jnp.float32)
    for block in range(BLOCKS):
        at = slice(block * 128, block * 128 + 128)
        x_blk = x_ref[:, at]
        dy_blk = dy_ref[:, at]
        parts = []
        for side in range(2):
            h = 2 * block + side
            diff = cum[h : h + 1, :] - columns[:, h : h + 1]
            weights = jnp.exp(jnp.where(later, diff, -1e30))
            x_side = jnp.where(first_lanes == (side == 0), x_blk, jnp.zeros_like(x_blk))
            pairs = pairs + dot(x_side, dy_blk, NT) * weights
            scores = (inner * weights).astype(jnp.bfloat16)
            parts.append(dot(scores, dy_blk, NN))
        local_x[:, at] = jnp.where(first_lanes, parts[0], parts[1])
    local_b[...] = dot(pairs.astype(jnp.bfloat16), c_blk, NN)
    local_c[...] = dot(jnp.transpose(pairs).astype(jnp.bfloat16), b_blk, NN)

    def exchange(src, dst, n):
        copy = pltpu.make_async_remote_copy(
            src_ref=src, dst_ref=dst, send_sem=send_sems.at[n], recv_sem=recv_sems.at[n],
            device_id=other_half, device_id_type=MESH,
        )
        copy.start()
        return copy

    wait_bytes(gain_in.at[pl.ds(0, GROUP - 1)], recv_sems, 0)
    wait_bytes(bwd_in.at[pl.ds(0, GROUP - 1)], recv_sems, 1)
    for l in range(LINES):
        gain_tot[l] = gain_in[2 * l] * gain_in[2 * l + 1]
        bwd_tot[l] = bwd_in[2 * l] + gain_in[2 * l] * bwd_in[2 * l + 1]
    gain_copy = exchange(gain_tot, gain_oth, 3)
    bwd_copy = exchange(bwd_tot, bwd_oth, 4)
    wait_bytes(fwd_in.at[pl.ds(0, GROUP - 1)], recv_sems, 2)
    for l in range(LINES):
        fwd_tot[l] = fwd_in[2 * l] * gain_in[2 * l + 1] + fwd_in[2 * l + 1]
    fwd_copy = exchange(fwd_tot, fwd_oth, 5)

    is_left = jnp.full((ROWS, 128), half) == 0

    gain_copy.wait()
    bwd_copy.wait()
    cur = jnp.zeros((ROWS, 128), jnp.float32)
    for l in reversed(range(LINES)):
        cur = jnp.where(is_left, bwd_oth[l] + gain_oth[l] * cur, cur)
        leave_out[2 * l + 1] = cur
        cur = bwd_in[2 * l + 1] + gain_in[2 * l + 1] * cur
        leave_out[2 * l] = cur
        cur = bwd_in[2 * l] + gain_in[2 * l] * cur
        cur = jnp.where(is_left, cur, bwd_oth[l] + gain_oth[l] * cur)
    scatter(leave_out, leave_in, 6)
    leave_in[mine] = leave_out[mine]

    fwd_copy.wait()
    cur = jnp.zeros((ROWS, 128), jnp.float32)
    for l in range(LINES):
        cur = jnp.where(is_left, cur, fwd_oth[l] + gain_oth[l] * cur)
        enter_out[2 * l] = cur
        cur = fwd_in[2 * l] + gain_in[2 * l] * cur
        enter_out[2 * l + 1] = cur
        cur = fwd_in[2 * l + 1] + gain_in[2 * l + 1] * cur
        cur = jnp.where(is_left, fwd_oth[l] + gain_oth[l] * cur, cur)
    scatter(enter_out, enter_in, 7)
    enter_in[mine] = enter_out[mine]

    wait_bytes(leave_in.at[pl.ds(0, GROUP - 1)], recv_sems, 6)
    sum_b = local_b[...]
    for block in range(BLOCKS):
        at = slice(block * 128, block * 128 + 128)
        leave = leave_in[block * 8 : block * 8 + 8].reshape(STATE, 128).astype(jnp.bfloat16)
        gx_ref[:, at] = (local_x[:, at] + end_ref[:, at] * dot(b_blk, leave, NN)).astype(jnp.bfloat16)
        sum_b = sum_b + dot(xs_ref[:, at], leave, NT)
    core_out[:, :, 0] = sum_b.reshape(4, 2, PART, 128)

    wait_bytes(enter_in.at[pl.ds(0, GROUP - 1)], recv_sems, 7)
    sum_c = local_c[...]
    for block in range(BLOCKS):
        at = slice(block * 128, block * 128 + 128)
        enter = enter_in[block * 8 : block * 8 + 8].reshape(STATE, 128).astype(jnp.bfloat16)
        sum_c = sum_c + dot(ys_ref[:, at], enter, NT)
    core_out[:, :, 1] = sum_c.reshape(4, 2, PART, 128)

    core_copy = pltpu.make_async_remote_copy(
        src_ref=core_out.at[:, 1 - core], dst_ref=core_in, send_sem=send_sems.at[8],
        recv_sem=recv_sems.at[8], device_id=other_core, device_id_type=MESH,
    )
    core_copy.start()
    core_copy.wait()
    part_out[...] = core_out[:, core] + core_in[...]
    copies = []
    for k in (2, 1, 3):
        to = lax.rem(z_hi + k, 4)
        copy = pltpu.make_async_remote_copy(
            src_ref=part_out.at[to], dst_ref=part_in.at[k - 1], send_sem=send_sems.at[8 + k],
            recv_sem=recv_sems.at[8 + k], device_id={"head": to * 2 + core}, device_id_type=MESH,
        )
        copy.start()
        copies.append(copy)
    for copy in copies:
        copy.wait()
    total = part_out[z_hi] + part_in[0] + part_in[1] + part_in[2]
    gb_ref[...] = total[0]
    gc_ref[...] = total[1]

    wait_bytes(gain_in.at[pl.ds(0, GROUP - 1)], send_sems, 0)
    for n, ref in ((1, bwd_in), (2, fwd_in), (6, leave_in), (7, enter_in)):
        wait_bytes(ref.at[pl.ds(0, GROUP - 1)], send_sems, n)


def on_device(x_seq, grad_out, b_proj, c_proj, decay_rate):
    def vmem(shape, dtype=jnp.float32):
        return pltpu.VMEM(shape, dtype)

    chunks = (GROUP, ROWS, 128)
    totals = (LINES, ROWS, 128)
    return pl.pallas_call(
        kernel,
        out_shape=(
            jax.ShapeDtypeStruct((Q, HEADS * WIDTH), jnp.bfloat16),
            jax.ShapeDtypeStruct((PART, STATE), jnp.float32),
            jax.ShapeDtypeStruct((PART, STATE), jnp.float32),
        ),
        in_specs=[pl.BlockSpec(memory_space=pltpu.VMEM)] * 5,
        out_specs=(pl.BlockSpec(memory_space=pltpu.VMEM),) * 3,
        scratch_shapes=[
            vmem(chunks), vmem(chunks), vmem((BLOCKS, 1, 128)),
            vmem(chunks), vmem(chunks), vmem((GROUP, 1, 128)),
            vmem(totals), vmem(totals), vmem((LINES, 1, 128)),
            vmem(totals), vmem(totals), vmem((LINES, 1, 128)),
            vmem(chunks), vmem(chunks), vmem(chunks), vmem(chunks),
            vmem((Q, HEADS * WIDTH), jnp.bfloat16), vmem((Q, HEADS * WIDTH), jnp.bfloat16),
            vmem((Q, HEADS * WIDTH)), vmem((Q, HEADS * WIDTH)),
            vmem((Q, STATE)), vmem((Q, STATE)),
            vmem((4, 2, 2, PART, 128)), vmem((4, 2, PART, 128)),
            vmem((4, 2, PART, 128)), vmem((3, 2, PART, 128)),
            pltpu.SemaphoreType.DMA((12,)), pltpu.SemaphoreType.DMA((12,)),
        ],
        compiler_params=pltpu.CompilerParams(
            collective_id=0, has_side_effects=True, vmem_limit_bytes=40 << 20
        ),
    )(x_seq, grad_out, b_proj, c_proj, decay_rate)


def solution(mesh):
    placed = (P("ctx", "head"), P("ctx", "head"), P("ctx", None), P("ctx", None), P("head", "ctx"))
    return jax.shard_map(
        on_device,
        mesh=mesh,
        in_specs=placed,
        out_specs=(P("ctx", "head"), P(("ctx", "head"), None), P(("ctx", "head"), None)),
        check_vma=False,
    )
```

```python
import jax
import jax.numpy as jnp
from jax import lax
from jax.experimental import pallas as pl
from jax.experimental.pallas import tpu as pltpu
from jax.sharding import PartitionSpec as P

MESH = pl.DeviceIdType.MESH
Q = 256
HEADS = 8
WIDTH = 64
STATE = 128
BLOCKS = 4
GROUP = 32
ROWS = 16
LINES = 16
PART = 32
PIECES = 4

NN = (((1,), (0,)), ((), ()))
NT = (((1,), (1,)), ((), ()))
TN = (((0,), (0,)), ((), ()))


def dot(a, b, dims):
    return lax.dot_general(a, b, dims, preferred_element_type=jnp.float32)


def kernel(
    x_hbm, dy_hbm, b_hbm, c_hbm, decay_hbm,
    gx_hbm, gb_hbm, gc_hbm,
    x_ref, dy_ref, b_ref, c_ref, decay_ref, gx_ref, gb_ref, gc_ref,
    fwd_out, bwd_out, gain_out, fwd_in, bwd_in, gain_in,
    fwd_tot, bwd_tot, gain_tot, fwd_oth, bwd_oth, gain_oth,
    enter_out, leave_out, enter_in, leave_in,
    xs_ref, ys_ref, end_ref, local_x, local_b, local_c,
    core_out, core_in, part_out, part_in,
    in_sems, send_sems, recv_sems, fwd_sems, bwd_sems, mid_fwd_sems, mid_bwd_sems, mid_gain_sems,
    gain_sems, core_sems, part_send, part_recv, out_sems, ready,
):
    me = lax.axis_index("ctx")
    head = lax.axis_index("head")
    line = me // 4
    plane_of_me = me // 16
    half = (me // 2) % 2
    mine = line * 2 + me % 2
    core = head % 2
    z_hi = head // 2

    def ctx_of(i):
        return (i // 2) * 4 + half * 2 + i % 2

    other_half = {"ctx": line * 4 + (1 - half) * 2 + me % 2}
    other_core = {"head": z_hi * 2 + 1 - core}
    early = z_hi == 0

    loads = []
    for n, (src, dst) in enumerate((
        (decay_hbm, decay_ref), (c_hbm, c_ref), (b_hbm, b_ref), (dy_hbm, dy_ref), (x_hbm, x_ref)
    )):
        loads.append(pltpu.make_async_copy(src, dst, in_sems.at[n]))
        loads[-1].start()

    barrier = pltpu.get_barrier_semaphore()

    def greet(k, carry):
        pl.semaphore_signal(
            barrier, inc=1, device_id={"ctx": ctx_of(lax.rem(mine + k, GROUP))}, device_id_type=MESH
        )
        return carry

    lax.fori_loop(1, GROUP, greet, 0)
    pl.semaphore_signal(barrier, inc=1, device_id=other_half, device_id_type=MESH)
    pl.semaphore_signal(barrier, inc=1, device_id=other_core, device_id_type=MESH)
    def tell_later(sem):
        for k in range(1, 4):
            pl.semaphore_signal(sem, inc=1, device_id={"head": k * 2 + core}, device_id_type=MESH)

    @pl.when(early)
    def _():
        tell_later(barrier)

    loads[0].wait()
    lane = lax.broadcasted_iota(jnp.int32, (HEADS, Q), 1)
    cum = jnp.log(decay_ref[...])
    step = 1
    while step < Q:
        cum = cum + jnp.where(lane >= step, pltpu.roll(cum, step, 1), 0.0)
        step *= 2
    to_end = jnp.exp(cum[:, Q - 1 : Q] - cum)
    from_start = jnp.exp(cum)
    columns = jnp.transpose(jnp.concatenate([cum, to_end, from_start], axis=0))
    first_lanes = lax.broadcasted_iota(jnp.int32, (Q, 128), 1) < WIDTH
    for load in loads[1:]:
        load.wait()
    b_blk = b_ref[...]
    c_blk = c_ref[...]

    def spread(base, block):
        left = jnp.broadcast_to(columns[:, base + 2 * block : base + 2 * block + 1], (Q, 128))
        right = jnp.broadcast_to(columns[:, base + 2 * block + 1 : base + 2 * block + 2], (Q, 128))
        return jnp.where(first_lanes, left, right)

    for block in range(BLOCKS):
        at = slice(block * 128, block * 128 + 128)
        end_blk = spread(HEADS, block)
        start_blk = spread(2 * HEADS, block)
        end_ref[:, at] = end_blk
        xs = (x_ref[:, at].astype(jnp.float32) * end_blk).astype(jnp.bfloat16)
        ys = (dy_ref[:, at].astype(jnp.float32) * start_blk).astype(jnp.bfloat16)
        xs_ref[:, at] = xs
        ys_ref[:, at] = ys
        gain_out[block] = start_blk[Q - 1 : Q, :]
        bwd_out[block * 8 : block * 8 + 8] = dot(c_blk, ys, TN).reshape(8, ROWS, 128)
        fwd_out[block * 8 : block * 8 + 8] = dot(b_blk, xs, TN).reshape(8, ROWS, 128)

    pl.semaphore_wait(barrier, GROUP - 1 + 1 + 1 + jnp.where(early, 0, 1))

    def send_to(i, src, dst, send_sem, recv_sem):
        pltpu.make_async_remote_copy(
            src_ref=src, dst_ref=dst, send_sem=send_sem, recv_sem=recv_sem,
            device_id={"ctx": ctx_of(i)}, device_id_type=MESH,
        ).start()

    def scatter(out_of, into, send_sem, recv_sem):
        for k in (0, 1, 3, 2):
            first = lax.rem(plane_of_me + k, 4) * 8

            def one(j, carry, first=first):
                i = first + lax.rem(mine + j, 8)
                send_to(i, out_of(i), into.at[mine], send_sem, recv_sem)
                return carry

            lax.fori_loop(1 if k == 0 else 0, 8, one, 0)
        pltpu.make_async_copy(out_of(mine), into.at[mine], recv_sem).start()

    def wait_bytes(ref, sem):
        pltpu.make_async_copy(ref, ref, sem).wait()

    scatter(lambda i: gain_out.at[i // 8], gain_in, send_sems.at[0], gain_sems.at[plane_of_me])
    scatter(lambda i: bwd_out.at[i], bwd_in, send_sems.at[1], bwd_sems.at[plane_of_me])
    scatter(lambda i: fwd_out.at[i], fwd_in, send_sems.at[2], fwd_sems.at[plane_of_me])

    @pl.when(jnp.logical_not(early))
    def _():
        pl.semaphore_signal(ready, inc=1, device_id={"head": core}, device_id_type=MESH)

    def exchange(src, dst, send_sem, recv_sem):
        copy = pltpu.make_async_remote_copy(
            src_ref=src, dst_ref=dst, send_sem=send_sem, recv_sem=recv_sem,
            device_id=other_half, device_id_type=MESH,
        )
        copy.start()
        return copy

    copies = []
    for k in (0, 1, 3, 2):
        plane = lax.rem(plane_of_me + k, 4)
        sources = pl.ds(plane * 8, 8)
        at = pl.ds(plane * 4, 4)
        wait_bytes(gain_in.at[sources], gain_sems.at[plane])
        wait_bytes(bwd_in.at[sources], bwd_sems.at[plane])
        for j in range(4):
            l = plane * 4 + j
            gain_tot[l] = gain_in[2 * l] * gain_in[2 * l + 1]
            bwd_tot[l] = bwd_in[2 * l] + gain_in[2 * l] * bwd_in[2 * l + 1]
        exchange(gain_tot.at[at], gain_oth.at[at], send_sems.at[3], mid_gain_sems.at[plane])
        exchange(bwd_tot.at[at], bwd_oth.at[at], mid_bwd_sems.at[0, plane], mid_bwd_sems.at[1, plane])
    fwd_copies = []
    for plane in range(4):
        wait_bytes(fwd_in.at[plane * 8 : plane * 8 + 8], fwd_sems.at[plane])
        for l in range(plane * 4, plane * 4 + 4):
            fwd_tot[l] = fwd_in[2 * l] * gain_in[2 * l + 1] + fwd_in[2 * l + 1]
        at = slice(plane * 4, plane * 4 + 4)
        fwd_copies.append(exchange(fwd_tot.at[at], fwd_oth.at[at], mid_fwd_sems.at[0, plane], mid_fwd_sems.at[1, plane]))

    row = lax.broadcasted_iota(jnp.int32, (Q, Q), 0)
    col = lax.broadcasted_iota(jnp.int32, (Q, Q), 1)
    later = col >= row
    inner = dot(b_blk, c_blk, NT)
    pairs = jnp.zeros((Q, Q), jnp.float32)
    for block in range(BLOCKS):
        at = slice(block * 128, block * 128 + 128)
        x_blk = x_ref[:, at]
        dy_blk = dy_ref[:, at]
        parts = []
        for side in range(2):
            h = 2 * block + side
            diff = cum[h : h + 1, :] - columns[:, h : h + 1]
            weights = jnp.exp(jnp.where(later, diff, -1e30))
            x_side = jnp.where(first_lanes == (side == 0), x_blk, jnp.zeros_like(x_blk))
            pairs = pairs + dot(x_side, dy_blk, NT) * weights
            scores = (inner * weights).astype(jnp.bfloat16)
            parts.append(dot(scores, dy_blk, NN))
        local_x[:, at] = jnp.where(first_lanes, parts[0], parts[1])
    local_b[...] = dot(pairs.astype(jnp.bfloat16), c_blk, NN)
    local_c[...] = dot(jnp.transpose(pairs).astype(jnp.bfloat16), b_blk, NN)

    def send_back(out, into, plane, n):
        def one(k, carry):
            i = plane * 8 + lax.rem(mine + k, 8)

            @pl.when(i != mine)
            def _():
                send_to(i, out.at[i], into.at[mine], send_sems.at[n], recv_sems.at[n])

            @pl.when(i == mine)
            def _():
                pltpu.make_async_copy(out.at[mine], into.at[mine], recv_sems.at[n]).start()

            return carry

        lax.fori_loop(0, 8, one, 0)

    def send_all(out, into, n):
        def one(k, carry):
            i = lax.rem(mine + 13 * k, GROUP)
            send_to(i, out.at[i], into.at[mine], send_sems.at[n], recv_sems.at[n])
            return carry

        lax.fori_loop(1, GROUP, one, 0)
        pltpu.make_async_copy(out.at[mine], into.at[mine], recv_sems.at[n]).start()

    is_left = jnp.full((ROWS, 128), half) == 0
    cur = jnp.zeros((ROWS, 128), jnp.float32)
    for plane in reversed(range(4)):
        at = slice(plane * 4, plane * 4 + 4)
        wait_bytes(gain_oth.at[at], mid_gain_sems.at[plane])
        wait_bytes(bwd_oth.at[at], mid_bwd_sems.at[1, plane])
        for l in reversed(range(plane * 4, plane * 4 + 4)):
            cur = jnp.where(is_left, bwd_oth[l] + gain_oth[l] * cur, cur)
            leave_out[2 * l + 1] = cur
            cur = bwd_in[2 * l + 1] + gain_in[2 * l + 1] * cur
            leave_out[2 * l] = cur
            cur = bwd_in[2 * l] + gain_in[2 * l] * cur
            cur = jnp.where(is_left, cur, bwd_oth[l] + gain_oth[l] * cur)
        send_back(leave_out, leave_in, plane, 4)

    @pl.when(early)
    def _():
        pl.semaphore_wait(ready, 3)
        tell_later(ready)

    cur = jnp.zeros((ROWS, 128), jnp.float32)
    for plane in range(4):
        fwd_copies[plane].wait_recv()
        for l in range(plane * 4, plane * 4 + 4):
            cur = jnp.where(is_left, cur, fwd_oth[l] + gain_oth[l] * cur)
            enter_out[2 * l] = cur
            cur = fwd_in[2 * l] + gain_in[2 * l] * cur
            enter_out[2 * l + 1] = cur
            cur = fwd_in[2 * l + 1] + gain_in[2 * l + 1] * cur
            cur = jnp.where(is_left, fwd_oth[l] + gain_oth[l] * cur, cur)
    send_all(enter_out, enter_in, 5)

    def core_exchange(n, part, at):
        copy = pltpu.make_async_remote_copy(
            src_ref=core_out.at[n, at, 1 - core], dst_ref=core_in.at[n, at], send_sem=core_sems.at[0, n, part],
            recv_sem=core_sems.at[1, n, part], device_id=other_core, device_id_type=MESH,
        )
        copy.start()
        return copy

    def send_part(n, to):
        slot = z_hi - (z_hi > to).astype(jnp.int32)
        pltpu.make_async_remote_copy(
            src_ref=part_out.at[n, to], dst_ref=part_in.at[n, slot],
            send_sem=part_send.at[n], recv_sem=part_recv.at[n],
            device_id={"head": to * 2 + core}, device_id_type=MESH,
        ).start()

    def sum_heads(n, local, scaled_ref, state_in):
        states = [
            state_in[block * 8 : block * 8 + 8].reshape(STATE, 128).astype(jnp.bfloat16)
            for block in range(BLOCKS)
        ]
        pieces = (slice(0, 1), slice(1, 4))
        exchanges = []
        for part, at in enumerate(pieces):
            rows = slice(at.start * 2 * PART, at.stop * 2 * PART)
            total = local[rows]
            for block in range(BLOCKS):
                total = total + dot(scaled_ref[rows, block * 128 : block * 128 + 128], states[block], NT)
            core_out[n, at] = total.reshape(at.stop - at.start, 2, PART, 128)
            exchanges.append(core_exchange(n, part, at))
        if n == 0:
            @pl.when(jnp.logical_not(early))
            def _():
                pl.semaphore_wait(ready, 1)

        for part, at in enumerate(pieces):
            exchanges[part].wait_recv()
            part_out[n, at] = core_out[n, at, core] + core_in[n, at]
            for to in range(at.start, at.stop):
                @pl.when(z_hi != to)
                def _(to=to):
                    send_part(n, to)

        copies.extend(exchanges)
        return states

    wait_bytes(leave_in, recv_sems.at[4])
    leaves = sum_heads(0, local_b, xs_ref, leave_in)
    for block in range(BLOCKS):
        at = slice(block * 128, block * 128 + 128)
        gx_ref[:, at] = (local_x[:, at] + end_ref[:, at] * dot(b_blk, leaves[block], NN)).astype(jnp.bfloat16)
    stores = [pltpu.make_async_copy(gx_ref, gx_hbm, out_sems.at[0])]
    stores[0].start()

    wait_bytes(enter_in, recv_sems.at[5])
    sum_heads(1, local_c, ys_ref, enter_in)

    wait_bytes(gain_in.at[pl.ds(0, GROUP - 1)], send_sems.at[0])
    wait_bytes(gain_oth, send_sems.at[3])
    for n, ref in ((1, bwd_in), (2, fwd_in), (4, leave_in), (5, enter_in)):
        wait_bytes(ref.at[pl.ds(0, GROUP - 1)], send_sems.at[n])
    for plane in range(4):
        at = slice(plane * 4, plane * 4 + 4)
        wait_bytes(bwd_tot.at[at], mid_bwd_sems.at[0, plane])
        fwd_copies[plane].wait_send()

    for n, (out, out_hbm) in enumerate(((gb_ref, gb_hbm), (gc_ref, gc_hbm))):
        wait_bytes(part_in.at[n], part_recv.at[n])
        out[...] = part_out[n, z_hi] + part_in[n, 0] + part_in[n, 1] + part_in[n, 2]
        stores.append(pltpu.make_async_copy(out, out_hbm, out_sems.at[1 + n]))
        stores[-1].start()
    for n in range(2):
        wait_bytes(part_in.at[n], part_send.at[n])
        for part in range(2):
            copies[2 * n + part].wait_send()
    for store in stores:
        store.wait()


def place(gx_in, gb_in, gc_in, gx_out, gb_out, gc_out, gx_buf, gb_buf, gc_buf, in_sems, out_sems):
    rows = Q // PIECES
    parts = [(gx_in.at[at], gx_buf.at[at], gx_out.at[at]) for at in (pl.ds(n * rows, rows) for n in range(PIECES))]
    parts += [(gb_in, gb_buf, gb_out), (gc_in, gc_buf, gc_out)]
    loads = [pltpu.make_async_copy(src, buf, in_sems.at[n]) for n, (src, buf, dst) in enumerate(parts)]
    stores = [pltpu.make_async_copy(buf, dst, out_sems.at[n]) for n, (src, buf, dst) in enumerate(parts)]
    for load in loads:
        load.start()
    for load, store in zip(loads, stores):
        load.wait()
        store.start()
    for store in stores:
        store.wait()


def on_device(x_seq, grad_out, b_proj, c_proj, decay_rate):
    def vmem(shape, dtype=jnp.float32):
        return pltpu.VMEM(shape, dtype)

    def dma(*shape):
        return pltpu.SemaphoreType.DMA(shape)

    chunks = (GROUP, ROWS, 128)
    totals = (LINES, ROWS, 128)
    wide = (Q, HEADS * WIDTH)
    hbm = pl.BlockSpec(memory_space=pltpu.HBM)
    results = (
        jax.ShapeDtypeStruct(wide, jnp.bfloat16),
        jax.ShapeDtypeStruct((PART, STATE), jnp.float32),
        jax.ShapeDtypeStruct((PART, STATE), jnp.float32),
    )
    sums = pl.pallas_call(
        kernel,
        out_shape=results,
        in_specs=[hbm] * 5,
        out_specs=(hbm,) * 3,
        scratch_shapes=[
            vmem(wide, jnp.bfloat16), vmem(wide, jnp.bfloat16),
            vmem((Q, STATE), jnp.bfloat16), vmem((Q, STATE), jnp.bfloat16), vmem((HEADS, Q)),
            vmem(wide, jnp.bfloat16), vmem((PART, STATE)), vmem((PART, STATE)),
            vmem(chunks), vmem(chunks), vmem((BLOCKS, 1, 128)),
            vmem(chunks), vmem(chunks), vmem((GROUP, 1, 128)),
            vmem(totals), vmem(totals), vmem((LINES, 1, 128)),
            vmem(totals), vmem(totals), vmem((LINES, 1, 128)),
            vmem(chunks), vmem(chunks), vmem(chunks), vmem(chunks),
            vmem(wide, jnp.bfloat16), vmem(wide, jnp.bfloat16),
            vmem(wide), vmem(wide),
            vmem((Q, STATE)), vmem((Q, STATE)),
            vmem((2, 4, 2, PART, 128)), vmem((2, 4, PART, 128)),
            vmem((2, 4, PART, 128)), vmem((2, 3, PART, 128)),
            dma(5), dma(6), dma(6), dma(4), dma(4), dma(2, 4), dma(2, 4), dma(4),
            dma(4), dma(2, 2, 2), dma(2), dma(2), dma(3), pltpu.SemaphoreType.REGULAR,
        ],
        compiler_params=pltpu.CompilerParams(
            collective_id=0, has_side_effects=True, vmem_limit_bytes=56 << 20
        ),
    )(x_seq, grad_out, b_proj, c_proj, decay_rate)
    return pl.pallas_call(
        place,
        out_shape=results,
        in_specs=[hbm] * 3,
        out_specs=(hbm,) * 3,
        scratch_shapes=[
            vmem(wide, jnp.bfloat16), vmem((PART, STATE)), vmem((PART, STATE)),
            dma(PIECES + 2), dma(PIECES + 2),
        ],
        compiler_params=pltpu.CompilerParams(vmem_limit_bytes=56 << 20),
    )(*sums)


def solution(mesh):
    placed = (P("ctx", "head"), P("ctx", "head"), P("ctx", None), P("ctx", None), P("head", "ctx"))
    return jax.shard_map(
        on_device,
        mesh=mesh,
        in_specs=placed,
        out_specs=(P("ctx", "head"), P(("ctx", "head"), None), P(("ctx", "head"), None)),
        check_vma=False,
    )
```

```python
import jax
import jax.numpy as jnp
from jax import lax
from jax.experimental import pallas as pl
from jax.experimental.pallas import tpu as pltpu
from jax.sharding import PartitionSpec as P

MESH = pl.DeviceIdType.MESH
Q = 256
HEADS = 8
WIDTH = 64
STATE = 128
BLOCKS = 4
GROUP = 32
ROWS = 16
LINES = 16
HALF = 8
PART = 32
PIECES = 4

NN = (((1,), (0,)), ((), ()))
NT = (((1,), (1,)), ((), ()))
TN = (((0,), (0,)), ((), ()))


def dot(a, b, dims):
    return lax.dot_general(a, b, dims, preferred_element_type=jnp.float32)


def kernel(
    x_hbm, dy_hbm, b_hbm, c_hbm, decay_hbm,
    gx_hbm, gb_hbm, gc_hbm,
    x_ref, dy_ref, b_ref, c_ref, decay_ref, gx_ref, gb_ref, gc_ref,
    fwd_out, bwd_out, fwd_in, bwd_in,
    fwd_tot, bwd_tot, fwd_oth, bwd_oth,
    enter_out, leave_out, enter_in, leave_in,
    xs_ref, ys_ref, end_ref, local_x, local_b, local_c,
    core_out, core_in, part_out, part_in,
    in_sems, send_sems, recv_sems, fwd_sems, bwd_sems, mid_fwd_sems, mid_bwd_sems,
    core_sems, part_send, part_recv, out_sems, ready,
):
    me = lax.axis_index("ctx")
    head = lax.axis_index("head")
    line = me // 4
    plane_of_me = me // 16
    half = (me // 2) % 2
    mine = line * 2 + me % 2
    core = head % 2
    z_hi = head // 2

    def ctx_of(i):
        return (i // 2) * 4 + half * 2 + i % 2

    other_half = {"ctx": line * 4 + (1 - half) * 2 + me % 2}
    other_core = {"head": z_hi * 2 + 1 - core}
    early = z_hi == 0

    loads = []
    for n, (src, dst) in enumerate((
        (decay_hbm, decay_ref), (c_hbm, c_ref), (b_hbm, b_ref), (dy_hbm, dy_ref), (x_hbm, x_ref)
    )):
        loads.append(pltpu.make_async_copy(src, dst, in_sems.at[n]))
        loads[-1].start()

    barrier = pltpu.get_barrier_semaphore()

    def greet(k, carry):
        pl.semaphore_signal(
            barrier, inc=1, device_id={"ctx": ctx_of(lax.rem(mine + k, GROUP))}, device_id_type=MESH
        )
        return carry

    lax.fori_loop(1, GROUP, greet, 0)
    pl.semaphore_signal(barrier, inc=1, device_id=other_half, device_id_type=MESH)
    pl.semaphore_signal(barrier, inc=1, device_id=other_core, device_id_type=MESH)
    def tell_later(sem):
        for k in range(1, 4):
            pl.semaphore_signal(sem, inc=1, device_id={"head": k * 2 + core}, device_id_type=MESH)

    @pl.when(early)
    def _():
        tell_later(barrier)

    loads[0].wait()
    lane = lax.broadcasted_iota(jnp.int32, (HEADS, Q), 1)
    cum = jnp.log(decay_ref[...])
    step = 1
    while step < Q:
        cum = cum + jnp.where(lane >= step, pltpu.roll(cum, step, 1), 0.0)
        step *= 2
    to_end = jnp.exp(cum[:, Q - 1 : Q] - cum)
    from_start = jnp.exp(cum)
    columns = jnp.transpose(jnp.concatenate([cum, to_end, from_start], axis=0))
    first_lanes = lax.broadcasted_iota(jnp.int32, (Q, 128), 1) < WIDTH
    for load in loads[1:]:
        load.wait()
    b_blk = b_ref[...]
    c_blk = c_ref[...]

    def spread(base, block):
        left = jnp.broadcast_to(columns[:, base + 2 * block : base + 2 * block + 1], (Q, 128))
        right = jnp.broadcast_to(columns[:, base + 2 * block + 1 : base + 2 * block + 2], (Q, 128))
        return jnp.where(first_lanes, left, right)

    for block in range(BLOCKS):
        at = slice(block * 128, block * 128 + 128)
        end_blk = spread(HEADS, block)
        start_blk = spread(2 * HEADS, block)
        end_ref[:, at] = end_blk
        xs = (x_ref[:, at].astype(jnp.float32) * end_blk).astype(jnp.bfloat16)
        ys = (dy_ref[:, at].astype(jnp.float32) * start_blk).astype(jnp.bfloat16)
        xs_ref[:, at] = xs
        ys_ref[:, at] = ys
        bwd_out[block * 8 : block * 8 + 8, ROWS:] = jnp.broadcast_to(start_blk[Q - 1 : Q, :][None], (8, 1, 128))
        bwd_out[block * 8 : block * 8 + 8, :ROWS] = dot(c_blk, ys, TN).reshape(8, ROWS, 128)
        fwd_out[block * 8 : block * 8 + 8] = dot(b_blk, xs, TN).reshape(8, ROWS, 128)

    pl.semaphore_wait(barrier, GROUP - 1 + 1 + 1 + jnp.where(early, 0, 1))

    @pl.when(jnp.logical_not(early))
    def _():
        pl.semaphore_signal(ready, inc=1, device_id={"head": core}, device_id_type=MESH)

    def send_to(i, src, dst, send_sem, recv_sem):
        pltpu.make_async_remote_copy(
            src_ref=src, dst_ref=dst, send_sem=send_sem, recv_sem=recv_sem,
            device_id={"ctx": ctx_of(i)}, device_id_type=MESH,
        ).start()

    def scatter(out_of, into, send_sem, recv_sem):
        for k in (0, 1, 3, 2):
            first = lax.rem(plane_of_me + k, 4) * 8

            def one(j, carry, first=first):
                i = first + lax.rem(mine + j, 8)
                send_to(i, out_of(i), into.at[mine], send_sem, recv_sem)
                return carry

            lax.fori_loop(1 if k == 0 else 0, 8, one, 0)
        pltpu.make_async_copy(out_of(mine), into.at[mine], recv_sem).start()

    def wait_bytes(ref, sem):
        pltpu.make_async_copy(ref, ref, sem).wait()

    scatter(lambda i: bwd_out.at[i], bwd_in, send_sems.at[1], bwd_sems.at[plane_of_me])
    scatter(lambda i: fwd_out.at[i], fwd_in, send_sems.at[2], fwd_sems.at[plane_of_me])

    def exchange(src, dst, send_sem, recv_sem):
        copy = pltpu.make_async_remote_copy(
            src_ref=src, dst_ref=dst, send_sem=send_sem, recv_sem=recv_sem,
            device_id=other_half, device_id_type=MESH,
        )
        copy.start()
        return copy

    copies = []
    def gain_of(j):
        return bwd_in[j, ROWS:]

    def other_gain(l):
        return bwd_oth[l, ROWS:]

    for k in (0, 1, 3, 2):
        plane = lax.rem(plane_of_me + k, 4)
        sources = pl.ds(plane * 8, 8)
        at = pl.ds(plane * 4, 4)
        wait_bytes(bwd_in.at[sources], bwd_sems.at[plane])
        for j in range(4):
            l = plane * 4 + j
            first_gain = gain_of(2 * l)
            bwd_tot[l, :ROWS] = bwd_in[2 * l, :ROWS] + first_gain * bwd_in[2 * l + 1, :ROWS]
            bwd_tot[l, ROWS:] = first_gain * gain_of(2 * l + 1)
        exchange(bwd_tot.at[at], bwd_oth.at[at], mid_bwd_sems.at[0, plane], mid_bwd_sems.at[1, plane])
    for plane in range(4):
        wait_bytes(fwd_in.at[plane * 8 : plane * 8 + 8], fwd_sems.at[plane])
    fwd_copies = []
    for part in range(2):
        at = slice(part * HALF, part * HALF + HALF)
        for l in range(LINES):
            fwd_tot[part, l] = fwd_in[2 * l, at] * gain_of(2 * l + 1) + fwd_in[2 * l + 1, at]
        fwd_copies.append(
            exchange(fwd_tot.at[part], fwd_oth.at[part], mid_fwd_sems.at[0, part], mid_fwd_sems.at[1, part])
        )

    row = lax.broadcasted_iota(jnp.int32, (Q, Q), 0)
    col = lax.broadcasted_iota(jnp.int32, (Q, Q), 1)
    later = col >= row
    inner = dot(b_blk, c_blk, NT)
    pairs = jnp.zeros((Q, Q), jnp.float32)
    for block in range(BLOCKS):
        at = slice(block * 128, block * 128 + 128)
        x_blk = x_ref[:, at]
        dy_blk = dy_ref[:, at]
        parts = []
        for side in range(2):
            h = 2 * block + side
            diff = cum[h : h + 1, :] - columns[:, h : h + 1]
            weights = jnp.exp(jnp.where(later, diff, -1e30))
            x_side = jnp.where(first_lanes == (side == 0), x_blk, jnp.zeros_like(x_blk))
            pairs = pairs + dot(x_side, dy_blk, NT) * weights
            scores = (inner * weights).astype(jnp.bfloat16)
            parts.append(dot(scores, dy_blk, NN))
        local_x[:, at] = jnp.where(first_lanes, parts[0], parts[1])
    local_b[...] = dot(pairs.astype(jnp.bfloat16), c_blk, NN)
    local_c[...] = dot(jnp.transpose(pairs).astype(jnp.bfloat16), b_blk, NN)

    def send_back(out, into, plane, n):
        def one(k, carry):
            i = plane * 8 + lax.rem(mine + k, 8)

            @pl.when(i != mine)
            def _():
                send_to(i, out.at[i], into.at[mine], send_sems.at[n], recv_sems.at[n])

            @pl.when(i == mine)
            def _():
                pltpu.make_async_copy(out.at[mine], into.at[mine], recv_sems.at[n]).start()

            return carry

        lax.fori_loop(0, 8, one, 0)

    def send_all(out, into, at, n):
        slot = into.at[mine, at]

        def one(k, carry):
            i = lax.rem(mine + 13 * k, GROUP)
            send_to(i, out.at[i], slot, send_sems.at[n], recv_sems.at[n])
            return carry

        lax.fori_loop(1, GROUP, one, 0)
        pltpu.make_async_copy(out.at[mine], slot, recv_sems.at[n]).start()

    is_left = jnp.full((ROWS, 128), half) == 0
    cur = jnp.zeros((ROWS, 128), jnp.float32)
    for plane in reversed(range(4)):
        at = slice(plane * 4, plane * 4 + 4)
        wait_bytes(bwd_oth.at[at], mid_bwd_sems.at[1, plane])
        for l in reversed(range(plane * 4, plane * 4 + 4)):
            cur = jnp.where(is_left, bwd_oth[l, :ROWS] + other_gain(l) * cur, cur)
            leave_out[2 * l + 1] = cur
            cur = bwd_in[2 * l + 1, :ROWS] + gain_of(2 * l + 1) * cur
            leave_out[2 * l] = cur
            cur = bwd_in[2 * l, :ROWS] + gain_of(2 * l) * cur
            cur = jnp.where(is_left, cur, bwd_oth[l, :ROWS] + other_gain(l) * cur)
        send_back(leave_out, leave_in, plane, 4)

    @pl.when(early)
    def _():
        pl.semaphore_wait(ready, 3)
        tell_later(ready)

    for part in range(2):
        at = slice(part * HALF, part * HALF + HALF)
        left = is_left[at]
        cur = jnp.zeros((HALF, 128), jnp.float32)
        fwd_copies[part].wait_recv()
        for l in range(LINES):
            cur = jnp.where(left, cur, fwd_oth[part, l] + other_gain(l) * cur)
            enter_out[part, 2 * l] = cur
            cur = fwd_in[2 * l, at] + gain_of(2 * l) * cur
            enter_out[part, 2 * l + 1] = cur
            cur = fwd_in[2 * l + 1, at] + gain_of(2 * l + 1) * cur
            cur = jnp.where(left, fwd_oth[part, l] + other_gain(l) * cur, cur)
        send_all(enter_out.at[part], enter_in, at, 5)

    def core_exchange(n, part, at):
        copy = pltpu.make_async_remote_copy(
            src_ref=core_out.at[n, at, 1 - core], dst_ref=core_in.at[n, at], send_sem=core_sems.at[0, n, part],
            recv_sem=core_sems.at[1, n, part], device_id=other_core, device_id_type=MESH,
        )
        copy.start()
        return copy

    def send_part(n, to):
        slot = z_hi - (z_hi > to).astype(jnp.int32)
        pltpu.make_async_remote_copy(
            src_ref=part_out.at[n, to], dst_ref=part_in.at[n, slot],
            send_sem=part_send.at[n], recv_sem=part_recv.at[n],
            device_id={"head": to * 2 + core}, device_id_type=MESH,
        ).start()

    def sum_heads(n, local, scaled_ref, state_in):
        states = [
            state_in[block * 8 : block * 8 + 8].reshape(STATE, 128).astype(jnp.bfloat16)
            for block in range(BLOCKS)
        ]
        pieces = (slice(0, 1), slice(1, 4))
        exchanges = []
        for part, at in enumerate(pieces):
            rows = slice(at.start * 2 * PART, at.stop * 2 * PART)
            total = local[rows]
            for block in range(BLOCKS):
                total = total + dot(scaled_ref[rows, block * 128 : block * 128 + 128], states[block], NT)
            core_out[n, at] = total.reshape(at.stop - at.start, 2, PART, 128)
            exchanges.append(core_exchange(n, part, at))
        if n == 0:
            for block in range(BLOCKS):
                at = slice(block * 128, block * 128 + 128)
                carried = end_ref[:, at] * dot(b_blk, states[block], NN)
                gx_ref[:, at] = (local_x[:, at] + carried).astype(jnp.bfloat16)
        for part, at in enumerate(pieces):
            exchanges[part].wait_recv()
            part_out[n, at] = core_out[n, at, core] + core_in[n, at]
            if part == 0:
                @pl.when(jnp.logical_not(early))
                def _():
                    send_part(n, 0)

        copies.extend(exchanges)

    wait_bytes(leave_in, recv_sems.at[4])
    sum_heads(0, local_b, xs_ref, leave_in)
    stores = [pltpu.make_async_copy(gx_ref, gx_hbm, out_sems.at[0])]
    stores[0].start()

    wait_bytes(enter_in, recv_sems.at[5])
    sum_heads(1, local_c, ys_ref, enter_in)

    @pl.when(early)
    def _():
        wait_bytes(part_in.at[0], part_recv.at[0])

    @pl.when(jnp.logical_not(early))
    def _():
        pl.semaphore_wait(ready, 1)

    for n in range(2):
        for to in range(1, 4):
            @pl.when(z_hi != to)
            def _(n=n, to=to):
                send_part(n, to)

    @pl.when(jnp.logical_not(early))
    def _():
        wait_bytes(part_in.at[0], part_recv.at[0])


    for n, ref in ((1, bwd_in), (2, fwd_in), (4, leave_in), (5, enter_in)):
        wait_bytes(ref.at[pl.ds(0, GROUP - 1)], send_sems.at[n])
    for plane in range(4):
        at = slice(plane * 4, plane * 4 + 4)
        wait_bytes(bwd_tot.at[at], mid_bwd_sems.at[0, plane])
    for copy in fwd_copies:
        copy.wait_send()

    for n, (out, out_hbm) in enumerate(((gb_ref, gb_hbm), (gc_ref, gc_hbm))):
        if n == 1:
            wait_bytes(part_in.at[1], part_recv.at[1])
        out[...] = part_out[n, z_hi] + part_in[n, 0] + part_in[n, 1] + part_in[n, 2]
        stores.append(pltpu.make_async_copy(out, out_hbm, out_sems.at[1 + n]))
        stores[-1].start()
    for n in range(2):
        wait_bytes(part_in.at[n], part_send.at[n])
        for part in range(2):
            copies[2 * n + part].wait_send()
    for store in stores:
        store.wait()


def place(gx_in, gb_in, gc_in, gx_out, gb_out, gc_out, gx_buf, gb_buf, gc_buf, in_sems, out_sems):
    rows = Q // PIECES
    parts = [(gx_in.at[at], gx_buf.at[at], gx_out.at[at]) for at in (pl.ds(n * rows, rows) for n in range(PIECES))]
    parts += [(gb_in, gb_buf, gb_out), (gc_in, gc_buf, gc_out)]
    loads = [pltpu.make_async_copy(src, buf, in_sems.at[n]) for n, (src, buf, dst) in enumerate(parts)]
    stores = [pltpu.make_async_copy(buf, dst, out_sems.at[n]) for n, (src, buf, dst) in enumerate(parts)]
    for load in loads:
        load.start()
    for load, store in zip(loads, stores):
        load.wait()
        store.start()
    for store in stores:
        store.wait()


def on_device(x_seq, grad_out, b_proj, c_proj, decay_rate):
    def vmem(shape, dtype=jnp.float32):
        return pltpu.VMEM(shape, dtype)

    def dma(*shape):
        return pltpu.SemaphoreType.DMA(shape)

    chunks = (GROUP, ROWS, 128)
    totals = (2, LINES, HALF, 128)
    returns = (2, GROUP, HALF, 128)
    wide = (Q, HEADS * WIDTH)
    hbm = pl.BlockSpec(memory_space=pltpu.HBM)
    results = (
        jax.ShapeDtypeStruct(wide, jnp.bfloat16),
        jax.ShapeDtypeStruct((PART, STATE), jnp.float32),
        jax.ShapeDtypeStruct((PART, STATE), jnp.float32),
    )
    sums = pl.pallas_call(
        kernel,
        out_shape=results,
        in_specs=[hbm] * 5,
        out_specs=(hbm,) * 3,
        scratch_shapes=[
            vmem(wide, jnp.bfloat16), vmem(wide, jnp.bfloat16),
            vmem((Q, STATE), jnp.bfloat16), vmem((Q, STATE), jnp.bfloat16), vmem((HEADS, Q)),
            vmem(wide, jnp.bfloat16), vmem((PART, STATE)), vmem((PART, STATE)),
            vmem(chunks), vmem((GROUP, ROWS + 1, 128)), vmem(chunks), vmem((GROUP, ROWS + 1, 128)),
            vmem(totals), vmem((LINES, ROWS + 1, 128)), vmem(totals), vmem((LINES, ROWS + 1, 128)),
            vmem(returns), vmem(chunks), vmem(chunks), vmem(chunks),
            vmem(wide, jnp.bfloat16), vmem(wide, jnp.bfloat16),
            vmem(wide), vmem(wide),
            vmem((Q, STATE)), vmem((Q, STATE)),
            vmem((2, 4, 2, PART, 128)), vmem((2, 4, PART, 128)),
            vmem((2, 4, PART, 128)), vmem((2, 3, PART, 128)),
            dma(5), dma(6), dma(6), dma(4), dma(4), dma(2, 2), dma(2, 4),
            dma(2, 2, 2), dma(2), dma(2), dma(3), pltpu.SemaphoreType.REGULAR,
        ],
        compiler_params=pltpu.CompilerParams(
            collective_id=0, has_side_effects=True, vmem_limit_bytes=56 << 20
        ),
    )(x_seq, grad_out, b_proj, c_proj, decay_rate)
    return pl.pallas_call(
        place,
        out_shape=results,
        in_specs=[hbm] * 3,
        out_specs=(hbm,) * 3,
        scratch_shapes=[
            vmem(wide, jnp.bfloat16), vmem((PART, STATE)), vmem((PART, STATE)),
            dma(PIECES + 2), dma(PIECES + 2),
        ],
        compiler_params=pltpu.CompilerParams(vmem_limit_bytes=56 << 20),
    )(*sums)


def solution(mesh):
    placed = (P("ctx", "head"), P("ctx", "head"), P("ctx", None), P("ctx", None), P("head", "ctx"))
    return jax.shard_map(
        on_device,
        mesh=mesh,
        in_specs=placed,
        out_specs=(P("ctx", "head"), P(("ctx", "head"), None), P(("ctx", "head"), None)),
        check_vma=False,
    )
```

```python
import jax
import jax.numpy as jnp
from jax import lax
from jax.experimental import pallas as pl
from jax.experimental.pallas import tpu as pltpu
from jax.sharding import PartitionSpec as P

MESH = pl.DeviceIdType.MESH
Q = 256
HEADS = 8
WIDTH = 64
STATE = 128
BLOCKS = 4
GROUP = 32
ROWS = 16
LINES = 16
HALF = 8
PART = 32
PIECES = 4

NN = (((1,), (0,)), ((), ()))
NT = (((1,), (1,)), ((), ()))
TN = (((0,), (0,)), ((), ()))


def dot(a, b, dims):
    return lax.dot_general(a, b, dims, preferred_element_type=jnp.float32)


def kernel(
    x_hbm, dy_hbm, b_hbm, c_hbm, decay_hbm,
    gx_hbm, gb_hbm, gc_hbm,
    x_ref, dy_ref, b_ref, c_ref, decay_ref, gx_ref, gb_ref, gc_ref,
    fwd_out, bwd_out, fwd_in, bwd_in,
    fwd_tot, bwd_tot, fwd_oth, bwd_oth,
    enter_out, leave_out, enter_in, leave_in,
    xs_ref, ys_ref, end_ref, local_x, local_b, local_c,
    core_out, core_in, part_out, part_in,
    in_sems, send_sems, recv_sems, fwd_sems, bwd_sems, mid_fwd_sems, mid_bwd_sems,
    core_sems, part_send, part_recv, out_sems, ready,
):
    me = lax.axis_index("ctx")
    head = lax.axis_index("head")
    line = me // 4
    plane_of_me = me // 16
    half = (me // 2) % 2
    mine = line * 2 + me % 2
    core = head % 2
    z_hi = head // 2

    def ctx_of(i):
        return (i // 2) * 4 + half * 2 + i % 2

    other_half = {"ctx": line * 4 + (1 - half) * 2 + me % 2}
    other_core = {"head": z_hi * 2 + 1 - core}
    early = z_hi == 0

    loads = []
    for n, (src, dst) in enumerate((
        (decay_hbm, decay_ref), (c_hbm, c_ref), (b_hbm, b_ref), (dy_hbm, dy_ref), (x_hbm, x_ref)
    )):
        loads.append(pltpu.make_async_copy(src, dst, in_sems.at[n]))
        loads[-1].start()

    barrier = pltpu.get_barrier_semaphore()

    def greet(k, carry):
        pl.semaphore_signal(
            barrier, inc=1, device_id={"ctx": ctx_of(lax.rem(mine + 13 * k, GROUP))}, device_id_type=MESH
        )
        return carry

    lax.fori_loop(1, GROUP, greet, 0, unroll=True)
    pl.semaphore_signal(barrier, inc=1, device_id=other_half, device_id_type=MESH)
    pl.semaphore_signal(barrier, inc=1, device_id=other_core, device_id_type=MESH)
    def tell_later(sem):
        for k in range(1, 4):
            pl.semaphore_signal(sem, inc=1, device_id={"head": k * 2 + core}, device_id_type=MESH)

    @pl.when(early)
    def _():
        tell_later(barrier)

    loads[0].wait()
    lane = lax.broadcasted_iota(jnp.int32, (HEADS, Q), 1)
    cum = jnp.log(decay_ref[...])
    step = 1
    while step < Q:
        cum = cum + jnp.where(lane >= step, pltpu.roll(cum, step, 1), 0.0)
        step *= 2
    to_end = jnp.exp(cum[:, Q - 1 : Q] - cum)
    from_start = jnp.exp(cum)
    columns = jnp.transpose(jnp.concatenate([cum, to_end, from_start], axis=0))
    first_lanes = lax.broadcasted_iota(jnp.int32, (Q, 128), 1) < WIDTH
    for load in loads[1:]:
        load.wait()
    b_blk = b_ref[...]
    c_blk = c_ref[...]

    def spread(base, block):
        left = jnp.broadcast_to(columns[:, base + 2 * block : base + 2 * block + 1], (Q, 128))
        right = jnp.broadcast_to(columns[:, base + 2 * block + 1 : base + 2 * block + 2], (Q, 128))
        return jnp.where(first_lanes, left, right)

    for block in range(BLOCKS):
        at = slice(block * 128, block * 128 + 128)
        end_blk = spread(HEADS, block)
        start_blk = spread(2 * HEADS, block)
        end_ref[:, at] = end_blk
        xs = (x_ref[:, at].astype(jnp.float32) * end_blk).astype(jnp.bfloat16)
        ys = (dy_ref[:, at].astype(jnp.float32) * start_blk).astype(jnp.bfloat16)
        xs_ref[:, at] = xs
        ys_ref[:, at] = ys
        bwd_out[block * 8 : block * 8 + 8, ROWS:] = jnp.broadcast_to(start_blk[Q - 1 : Q, :][None], (8, 1, 128))
        bwd_out[block * 8 : block * 8 + 8, :ROWS] = dot(c_blk, ys, TN).reshape(8, ROWS, 128)
        fwd_out[block * 8 : block * 8 + 8] = dot(b_blk, xs, TN).reshape(8, ROWS, 128)

    pl.semaphore_wait(barrier, GROUP - 1 + 1 + 1 + jnp.where(early, 0, 1))

    @pl.when(jnp.logical_not(early))
    def _():
        pl.semaphore_signal(ready, inc=1, device_id={"head": core}, device_id_type=MESH)

    def send_to(i, src, dst, send_sem, recv_sem):
        pltpu.make_async_remote_copy(
            src_ref=src, dst_ref=dst, send_sem=send_sem, recv_sem=recv_sem,
            device_id={"ctx": ctx_of(i)}, device_id_type=MESH,
        ).start()

    def scatter(out_of, into, send_sem, recv_sem):
        for k in (0, 1, 3, 2):
            first = lax.rem(plane_of_me + k, 4) * 8

            def one(j, carry, first=first):
                i = first + lax.rem(mine + j, 8)
                send_to(i, out_of(i), into.at[mine], send_sem, recv_sem)
                return carry

            lax.fori_loop(1 if k == 0 else 0, 8, one, 0, unroll=True)
        pltpu.make_async_copy(out_of(mine), into.at[mine], recv_sem).start()

    def wait_bytes(ref, sem):
        pltpu.make_async_copy(ref, ref, sem).wait()

    scatter(lambda i: bwd_out.at[i], bwd_in, send_sems.at[1], bwd_sems.at[plane_of_me])
    scatter(lambda i: fwd_out.at[i], fwd_in, send_sems.at[2], fwd_sems.at[plane_of_me])

    def exchange(src, dst, send_sem, recv_sem):
        copy = pltpu.make_async_remote_copy(
            src_ref=src, dst_ref=dst, send_sem=send_sem, recv_sem=recv_sem,
            device_id=other_half, device_id_type=MESH,
        )
        copy.start()
        return copy

    copies = []
    def gain_of(j):
        return bwd_in[j, ROWS:]

    def other_gain(l):
        return bwd_oth[l, ROWS:]

    for k in (0, 1, 3, 2):
        plane = lax.rem(plane_of_me + k, 4)
        sources = pl.ds(plane * 8, 8)
        at = pl.ds(plane * 4, 4)
        wait_bytes(bwd_in.at[sources], bwd_sems.at[plane])
        for j in range(4):
            l = plane * 4 + j
            first_gain = gain_of(2 * l)
            bwd_tot[l, :ROWS] = bwd_in[2 * l, :ROWS] + first_gain * bwd_in[2 * l + 1, :ROWS]
            bwd_tot[l, ROWS:] = first_gain * gain_of(2 * l + 1)
        exchange(bwd_tot.at[at], bwd_oth.at[at], mid_bwd_sems.at[0, plane], mid_bwd_sems.at[1, plane])
    for plane in range(4):
        wait_bytes(fwd_in.at[plane * 8 : plane * 8 + 8], fwd_sems.at[plane])
    fwd_copies = []
    for part in range(2):
        at = slice(part * HALF, part * HALF + HALF)
        for l in range(LINES):
            fwd_tot[part, l] = fwd_in[2 * l, at] * gain_of(2 * l + 1) + fwd_in[2 * l + 1, at]
        fwd_copies.append(
            exchange(fwd_tot.at[part], fwd_oth.at[part], mid_fwd_sems.at[0, part], mid_fwd_sems.at[1, part])
        )

    row = lax.broadcasted_iota(jnp.int32, (Q, Q), 0)
    col = lax.broadcasted_iota(jnp.int32, (Q, Q), 1)
    later = col >= row
    inner = dot(b_blk, c_blk, NT)
    pairs = jnp.zeros((Q, Q), jnp.float32)
    for block in range(BLOCKS):
        at = slice(block * 128, block * 128 + 128)
        x_blk = x_ref[:, at]
        dy_blk = dy_ref[:, at]
        parts = []
        for side in range(2):
            h = 2 * block + side
            diff = cum[h : h + 1, :] - columns[:, h : h + 1]
            weights = jnp.exp(jnp.where(later, diff, -1e30))
            x_side = jnp.where(first_lanes == (side == 0), x_blk, jnp.zeros_like(x_blk))
            pairs = pairs + dot(x_side, dy_blk, NT) * weights
            scores = (inner * weights).astype(jnp.bfloat16)
            parts.append(dot(scores, dy_blk, NN))
        local_x[:, at] = jnp.where(first_lanes, parts[0], parts[1])
    local_b[...] = dot(pairs.astype(jnp.bfloat16), c_blk, NN)
    local_c[...] = dot(jnp.transpose(pairs).astype(jnp.bfloat16), b_blk, NN)

    def send_back(out, into, plane, n):
        def one(k, carry):
            i = plane * 8 + lax.rem(mine + k, 8)

            @pl.when(i != mine)
            def _():
                send_to(i, out.at[i], into.at[mine], send_sems.at[n], recv_sems.at[n])

            @pl.when(i == mine)
            def _():
                pltpu.make_async_copy(out.at[mine], into.at[mine], recv_sems.at[n]).start()

            return carry

        lax.fori_loop(0, 8, one, 0)

    def send_all(out, into, at, n):
        slot = into.at[mine, at]

        def one(k, carry):
            i = lax.rem(mine + 13 * k, GROUP)
            send_to(i, out.at[i], slot, send_sems.at[n], recv_sems.at[n])
            return carry

        lax.fori_loop(1, GROUP, one, 0, unroll=True)
        pltpu.make_async_copy(out.at[mine], slot, recv_sems.at[n]).start()

    is_left = jnp.full((ROWS, 128), half) == 0
    cur = jnp.zeros((ROWS, 128), jnp.float32)
    for plane in reversed(range(4)):
        at = slice(plane * 4, plane * 4 + 4)
        wait_bytes(bwd_oth.at[at], mid_bwd_sems.at[1, plane])
        for l in reversed(range(plane * 4, plane * 4 + 4)):
            cur = jnp.where(is_left, bwd_oth[l, :ROWS] + other_gain(l) * cur, cur)
            leave_out[2 * l + 1] = cur
            cur = bwd_in[2 * l + 1, :ROWS] + gain_of(2 * l + 1) * cur
            leave_out[2 * l] = cur
            cur = bwd_in[2 * l, :ROWS] + gain_of(2 * l) * cur
            cur = jnp.where(is_left, cur, bwd_oth[l, :ROWS] + other_gain(l) * cur)
        send_back(leave_out, leave_in, plane, 4)

    @pl.when(early)
    def _():
        pl.semaphore_wait(ready, 3)
        tell_later(ready)

    for part in range(2):
        at = slice(part * HALF, part * HALF + HALF)
        left = is_left[at]
        cur = jnp.zeros((HALF, 128), jnp.float32)
        fwd_copies[part].wait_recv()
        for l in range(LINES):
            cur = jnp.where(left, cur, fwd_oth[part, l] + other_gain(l) * cur)
            enter_out[part, 2 * l] = cur
            cur = fwd_in[2 * l, at] + gain_of(2 * l) * cur
            enter_out[part, 2 * l + 1] = cur
            cur = fwd_in[2 * l + 1, at] + gain_of(2 * l + 1) * cur
            cur = jnp.where(left, fwd_oth[part, l] + other_gain(l) * cur, cur)
        send_all(enter_out.at[part], enter_in, at, 5)

    def core_exchange(n, part, at):
        copy = pltpu.make_async_remote_copy(
            src_ref=core_out.at[n, at, 1 - core], dst_ref=core_in.at[n, at], send_sem=core_sems.at[0, n, part],
            recv_sem=core_sems.at[1, n, part], device_id=other_core, device_id_type=MESH,
        )
        copy.start()
        return copy

    def send_part(n, to):
        slot = z_hi - (z_hi > to).astype(jnp.int32)
        pltpu.make_async_remote_copy(
            src_ref=part_out.at[n, to], dst_ref=part_in.at[n, slot],
            send_sem=part_send.at[n], recv_sem=part_recv.at[n],
            device_id={"head": to * 2 + core}, device_id_type=MESH,
        ).start()

    def sum_heads(n, local, scaled_ref, state_in):
        states = [
            state_in[block * 8 : block * 8 + 8].reshape(STATE, 128).astype(jnp.bfloat16)
            for block in range(BLOCKS)
        ]
        pieces = (slice(0, 1), slice(1, 4))
        exchanges = []
        for part, at in enumerate(pieces):
            rows = slice(at.start * 2 * PART, at.stop * 2 * PART)
            total = local[rows]
            for block in range(BLOCKS):
                total = total + dot(scaled_ref[rows, block * 128 : block * 128 + 128], states[block], NT)
            core_out[n, at] = total.reshape(at.stop - at.start, 2, PART, 128)
            exchanges.append(core_exchange(n, part, at))
        def settle(part):
            at = pieces[part]
            exchanges[part].wait_recv()
            part_out[n, at] = core_out[n, at, core] + core_in[n, at]

        settle(0)

        @pl.when(jnp.logical_not(early))
        def _():
            send_part(n, 0)

        later_sums.append(settle)
        copies.extend(exchanges)

    wait_bytes(leave_in, recv_sems.at[4])
    later_sums = []
    sum_heads(0, local_b, xs_ref, leave_in)
    wait_bytes(enter_in, recv_sems.at[5])
    sum_heads(1, local_c, ys_ref, enter_in)
    for block in range(BLOCKS):
        at = slice(block * 128, block * 128 + 128)
        leave = leave_in[block * 8 : block * 8 + 8].reshape(STATE, 128).astype(jnp.bfloat16)
        gx_ref[:, at] = (local_x[:, at] + end_ref[:, at] * dot(b_blk, leave, NN)).astype(jnp.bfloat16)
    stores = [pltpu.make_async_copy(gx_ref, gx_hbm, out_sems.at[0])]
    stores[0].start()
    for settle in later_sums:
        settle(1)

    @pl.when(jnp.logical_not(early))
    def _():
        pl.semaphore_wait(ready, 1)

    for n in range(2):
        for to in range(1, 4):
            @pl.when(z_hi != to)
            def _(n=n, to=to):
                send_part(n, to)

    wait_bytes(part_in.at[0], part_recv.at[0])

    for n, ref in ((1, bwd_in), (2, fwd_in), (4, leave_in), (5, enter_in)):
        wait_bytes(ref.at[pl.ds(0, GROUP - 1)], send_sems.at[n])
    for plane in range(4):
        at = slice(plane * 4, plane * 4 + 4)
        wait_bytes(bwd_tot.at[at], mid_bwd_sems.at[0, plane])
    for copy in fwd_copies:
        copy.wait_send()

    for n, (out, out_hbm) in enumerate(((gb_ref, gb_hbm), (gc_ref, gc_hbm))):
        if n == 1:
            wait_bytes(part_in.at[1], part_recv.at[1])
        out[...] = part_out[n, z_hi] + part_in[n, 0] + part_in[n, 1] + part_in[n, 2]
        stores.append(pltpu.make_async_copy(out, out_hbm, out_sems.at[1 + n]))
        stores[-1].start()
    for n in range(2):
        wait_bytes(part_in.at[n], part_send.at[n])
        for part in range(2):
            copies[2 * n + part].wait_send()
    for store in stores:
        store.wait()


def place(gx_in, gb_in, gc_in, gx_out, gb_out, gc_out, gx_buf, gb_buf, gc_buf, in_sems, out_sems):
    rows = Q // PIECES
    parts = [(gx_in.at[at], gx_buf.at[at], gx_out.at[at]) for at in (pl.ds(n * rows, rows) for n in range(PIECES))]
    parts += [(gb_in, gb_buf, gb_out), (gc_in, gc_buf, gc_out)]
    loads = [pltpu.make_async_copy(src, buf, in_sems.at[n]) for n, (src, buf, dst) in enumerate(parts)]
    stores = [pltpu.make_async_copy(buf, dst, out_sems.at[n]) for n, (src, buf, dst) in enumerate(parts)]
    for load in loads:
        load.start()
    for load, store in zip(loads, stores):
        load.wait()
        store.start()
    for store in stores:
        store.wait()


def on_device(x_seq, grad_out, b_proj, c_proj, decay_rate):
    def vmem(shape, dtype=jnp.float32):
        return pltpu.VMEM(shape, dtype)

    def dma(*shape):
        return pltpu.SemaphoreType.DMA(shape)

    chunks = (GROUP, ROWS, 128)
    totals = (2, LINES, HALF, 128)
    returns = (2, GROUP, HALF, 128)
    wide = (Q, HEADS * WIDTH)
    hbm = pl.BlockSpec(memory_space=pltpu.HBM)
    results = (
        jax.ShapeDtypeStruct(wide, jnp.bfloat16),
        jax.ShapeDtypeStruct((PART, STATE), jnp.float32),
        jax.ShapeDtypeStruct((PART, STATE), jnp.float32),
    )
    sums = pl.pallas_call(
        kernel,
        out_shape=results,
        in_specs=[hbm] * 5,
        out_specs=(hbm,) * 3,
        scratch_shapes=[
            vmem(wide, jnp.bfloat16), vmem(wide, jnp.bfloat16),
            vmem((Q, STATE), jnp.bfloat16), vmem((Q, STATE), jnp.bfloat16), vmem((HEADS, Q)),
            vmem(wide, jnp.bfloat16), vmem((PART, STATE)), vmem((PART, STATE)),
            vmem(chunks), vmem((GROUP, ROWS + 1, 128)), vmem(chunks), vmem((GROUP, ROWS + 1, 128)),
            vmem(totals), vmem((LINES, ROWS + 1, 128)), vmem(totals), vmem((LINES, ROWS + 1, 128)),
            vmem(returns), vmem(chunks), vmem(chunks), vmem(chunks),
            vmem(wide, jnp.bfloat16), vmem(wide, jnp.bfloat16),
            vmem(wide), vmem(wide),
            vmem((Q, STATE)), vmem((Q, STATE)),
            vmem((2, 4, 2, PART, 128)), vmem((2, 4, PART, 128)),
            vmem((2, 4, PART, 128)), vmem((2, 3, PART, 128)),
            dma(5), dma(6), dma(6), dma(4), dma(4), dma(2, 2), dma(2, 4),
            dma(2, 2, 2), dma(2), dma(2), dma(3), pltpu.SemaphoreType.REGULAR,
        ],
        compiler_params=pltpu.CompilerParams(
            collective_id=0, has_side_effects=True, vmem_limit_bytes=56 << 20
        ),
    )(x_seq, grad_out, b_proj, c_proj, decay_rate)
    return pl.pallas_call(
        place,
        out_shape=results,
        in_specs=[hbm] * 3,
        out_specs=(hbm,) * 3,
        scratch_shapes=[
            vmem(wide, jnp.bfloat16), vmem((PART, STATE)), vmem((PART, STATE)),
            dma(PIECES + 2), dma(PIECES + 2),
        ],
        compiler_params=pltpu.CompilerParams(vmem_limit_bytes=56 << 20),
    )(*sums)


def solution(mesh):
    placed = (P("ctx", "head"), P("ctx", "head"), P("ctx", None), P("ctx", None), P("head", "ctx"))
    return jax.shard_map(
        on_device,
        mesh=mesh,
        in_specs=placed,
        out_specs=(P("ctx", "head"), P(("ctx", "head"), None), P(("ctx", "head"), None)),
        check_vma=False,
    )
```

```python
import jax
import jax.numpy as jnp
from jax import lax
from jax.experimental import pallas as pl
from jax.experimental.pallas import tpu as pltpu
from jax.sharding import PartitionSpec as P

MESH = pl.DeviceIdType.MESH
Q = 256
HEADS = 8
WIDTH = 64
STATE = 128
BLOCKS = 4
GROUP = 32
ROWS = 16
LINES = 16
HALF = 8
PART = 32
PIECES = 4

NN = (((1,), (0,)), ((), ()))
NT = (((1,), (1,)), ((), ()))
TN = (((0,), (0,)), ((), ()))


def dot(a, b, dims):
    return lax.dot_general(a, b, dims, preferred_element_type=jnp.float32)


def kernel(
    x_hbm, dy_hbm, b_hbm, c_hbm, decay_hbm,
    gx_hbm, gb_hbm, gc_hbm,
    x_ref, dy_ref, b_ref, c_ref, decay_ref, gx_ref, gb_ref, gc_ref,
    fwd_out, bwd_out, fwd_in, bwd_in,
    fwd_tot, bwd_tot, fwd_oth, bwd_oth,
    enter_out, leave_out, enter_in, leave_in,
    xs_ref, ys_ref, end_ref, local_x, local_b, local_c,
    core_out, core_in, part_out, part_in,
    in_sems, send_sems, recv_sems, fwd_sems, bwd_sems, mid_fwd_sems, mid_bwd_sems,
    core_sems, part_send, part_recv, out_sems, ready,
):
    me = lax.axis_index("ctx")
    head = lax.axis_index("head")
    line = me // 4
    plane_of_me = me // 16
    half = (me // 2) % 2
    mine = line * 2 + me % 2
    core = head % 2
    z_hi = head // 2

    def ctx_of(i):
        return (i // 2) * 4 + half * 2 + i % 2

    other_half = {"ctx": line * 4 + (1 - half) * 2 + me % 2}
    other_core = {"head": z_hi * 2 + 1 - core}
    early = z_hi == 0

    loads = []
    for n, (src, dst) in enumerate((
        (decay_hbm, decay_ref), (c_hbm, c_ref), (b_hbm, b_ref), (dy_hbm, dy_ref), (x_hbm, x_ref)
    )):
        loads.append(pltpu.make_async_copy(src, dst, in_sems.at[n]))
        loads[-1].start()

    barrier = pltpu.get_barrier_semaphore()

    def greet(k, carry):
        pl.semaphore_signal(
            barrier, inc=1, device_id={"ctx": ctx_of(lax.rem(mine + 13 * k, GROUP))}, device_id_type=MESH
        )
        return carry

    lax.fori_loop(1, GROUP, greet, 0, unroll=True)
    pl.semaphore_signal(barrier, inc=1, device_id=other_half, device_id_type=MESH)
    pl.semaphore_signal(barrier, inc=1, device_id=other_core, device_id_type=MESH)
    def tell_later(sem):
        for k in range(1, 4):
            pl.semaphore_signal(sem, inc=1, device_id={"head": k * 2 + core}, device_id_type=MESH)

    @pl.when(early)
    def _():
        tell_later(barrier)

    loads[0].wait()
    lane = lax.broadcasted_iota(jnp.int32, (HEADS, Q), 1)
    cum = jnp.log(decay_ref[...])
    step = 1
    while step < Q:
        cum = cum + jnp.where(lane >= step, pltpu.roll(cum, step, 1), 0.0)
        step *= 2
    to_end = jnp.exp(cum[:, Q - 1 : Q] - cum)
    from_start = jnp.exp(cum)
    columns = jnp.transpose(jnp.concatenate([cum, to_end, from_start], axis=0))
    first_lanes = lax.broadcasted_iota(jnp.int32, (Q, 128), 1) < WIDTH
    for load in loads[1:]:
        load.wait()
    b_blk = b_ref[...]
    c_blk = c_ref[...]

    def spread(base, block):
        left = jnp.broadcast_to(columns[:, base + 2 * block : base + 2 * block + 1], (Q, 128))
        right = jnp.broadcast_to(columns[:, base + 2 * block + 1 : base + 2 * block + 2], (Q, 128))
        return jnp.where(first_lanes, left, right)

    for block in range(BLOCKS):
        at = slice(block * 128, block * 128 + 128)
        end_blk = spread(HEADS, block)
        start_blk = spread(2 * HEADS, block)
        end_ref[:, at] = end_blk
        xs = (x_ref[:, at].astype(jnp.float32) * end_blk).astype(jnp.bfloat16)
        ys = (dy_ref[:, at].astype(jnp.float32) * start_blk).astype(jnp.bfloat16)
        xs_ref[:, at] = xs
        ys_ref[:, at] = ys
        bwd_out[block * 8 : block * 8 + 8, ROWS:] = jnp.broadcast_to(start_blk[Q - 1 : Q, :][None], (8, 1, 128))
        bwd_out[block * 8 : block * 8 + 8, :ROWS] = dot(c_blk, ys, TN).reshape(8, ROWS, 128)
        fwd_out[block * 8 : block * 8 + 8] = dot(b_blk, xs, TN).reshape(8, ROWS, 128)

    pl.semaphore_wait(barrier, GROUP - 1 + 1 + 1 + jnp.where(early, 0, 1))

    @pl.when(jnp.logical_not(early))
    def _():
        pl.semaphore_signal(ready, inc=1, device_id={"head": core}, device_id_type=MESH)

    def send_to(i, src, dst, send_sem, recv_sem):
        pltpu.make_async_remote_copy(
            src_ref=src, dst_ref=dst, send_sem=send_sem, recv_sem=recv_sem,
            device_id={"ctx": ctx_of(i)}, device_id_type=MESH,
        ).start()

    def scatter(out_of, into, send_sem, recv_sem):
        for k in (0, 1, 3, 2):
            first = lax.rem(plane_of_me + k, 4) * 8

            def one(j, carry, first=first):
                i = first + lax.rem(mine + j, 8)
                send_to(i, out_of(i), into.at[mine], send_sem, recv_sem)
                return carry

            lax.fori_loop(1 if k == 0 else 0, 8, one, 0, unroll=True)
        pltpu.make_async_copy(out_of(mine), into.at[mine], recv_sem).start()

    def wait_bytes(ref, sem):
        pltpu.make_async_copy(ref, ref, sem).wait()

    scatter(lambda i: bwd_out.at[i], bwd_in, send_sems.at[1], bwd_sems.at[plane_of_me])
    def send_fwd(k, carry):
        i = lax.rem(mine + 13 * k, GROUP)
        send_to(i, fwd_out.at[i], fwd_in.at[mine], send_sems.at[2], fwd_sems.at[plane_of_me])
        return carry

    lax.fori_loop(1, GROUP, send_fwd, 0, unroll=True)
    pltpu.make_async_copy(fwd_out.at[mine], fwd_in.at[mine], fwd_sems.at[plane_of_me]).start()

    def exchange(src, dst, send_sem, recv_sem):
        copy = pltpu.make_async_remote_copy(
            src_ref=src, dst_ref=dst, send_sem=send_sem, recv_sem=recv_sem,
            device_id=other_half, device_id_type=MESH,
        )
        copy.start()
        return copy

    copies = []
    def gain_of(j):
        return bwd_in[j, ROWS:]

    def other_gain(l):
        return bwd_oth[l, ROWS:]

    for k in (0, 1, 3, 2):
        plane = lax.rem(plane_of_me + k, 4)
        sources = pl.ds(plane * 8, 8)
        at = pl.ds(plane * 4, 4)
        wait_bytes(bwd_in.at[sources], bwd_sems.at[plane])
        for j in range(4):
            l = plane * 4 + j
            first_gain = gain_of(2 * l)
            bwd_tot[l, :ROWS] = bwd_in[2 * l, :ROWS] + first_gain * bwd_in[2 * l + 1, :ROWS]
            bwd_tot[l, ROWS:] = first_gain * gain_of(2 * l + 1)
        exchange(bwd_tot.at[at], bwd_oth.at[at], mid_bwd_sems.at[0, plane], mid_bwd_sems.at[1, plane])
    for plane in range(4):
        wait_bytes(fwd_in.at[plane * 8 : plane * 8 + 8], fwd_sems.at[plane])
    fwd_copies = []
    for part in range(2):
        at = slice(part * HALF, part * HALF + HALF)
        for l in range(LINES):
            fwd_tot[part, l] = fwd_in[2 * l, at] * gain_of(2 * l + 1) + fwd_in[2 * l + 1, at]
        fwd_copies.append(
            exchange(fwd_tot.at[part], fwd_oth.at[part], mid_fwd_sems.at[0, part], mid_fwd_sems.at[1, part])
        )

    row = lax.broadcasted_iota(jnp.int32, (Q, Q), 0)
    col = lax.broadcasted_iota(jnp.int32, (Q, Q), 1)
    later = col >= row
    inner = dot(b_blk, c_blk, NT)
    pairs = jnp.zeros((Q, Q), jnp.float32)
    for block in range(BLOCKS):
        at = slice(block * 128, block * 128 + 128)
        x_blk = x_ref[:, at]
        dy_blk = dy_ref[:, at]
        parts = []
        for side in range(2):
            h = 2 * block + side
            diff = cum[h : h + 1, :] - columns[:, h : h + 1]
            weights = jnp.exp(jnp.where(later, diff, -1e30))
            x_side = jnp.where(first_lanes == (side == 0), x_blk, jnp.zeros_like(x_blk))
            pairs = pairs + dot(x_side, dy_blk, NT) * weights
            scores = (inner * weights).astype(jnp.bfloat16)
            parts.append(dot(scores, dy_blk, NN))
        local_x[:, at] = jnp.where(first_lanes, parts[0], parts[1])
    local_b[...] = dot(pairs.astype(jnp.bfloat16), c_blk, NN)
    local_c[...] = dot(jnp.transpose(pairs).astype(jnp.bfloat16), b_blk, NN)

    def send_back(out, into, plane, n):
        def one(k, carry):
            i = plane * 8 + lax.rem(mine + k, 8)

            @pl.when(i != mine)
            def _():
                send_to(i, out.at[i], into.at[mine], send_sems.at[n], recv_sems.at[n])

            @pl.when(i == mine)
            def _():
                pltpu.make_async_copy(out.at[mine], into.at[mine], recv_sems.at[n]).start()

            return carry

        lax.fori_loop(0, 8, one, 0)

    def send_all(out, into, at, n):
        slot = into.at[mine, at]

        def one(k, carry):
            i = lax.rem(mine + 13 * k, GROUP)
            send_to(i, out.at[i], slot, send_sems.at[n], recv_sems.at[n])
            return carry

        lax.fori_loop(1, GROUP, one, 0, unroll=True)
        pltpu.make_async_copy(out.at[mine], slot, recv_sems.at[n]).start()

    is_left = jnp.full((ROWS, 128), half) == 0
    cur = jnp.zeros((ROWS, 128), jnp.float32)
    for plane in reversed(range(4)):
        at = slice(plane * 4, plane * 4 + 4)
        wait_bytes(bwd_oth.at[at], mid_bwd_sems.at[1, plane])
        for l in reversed(range(plane * 4, plane * 4 + 4)):
            cur = jnp.where(is_left, bwd_oth[l, :ROWS] + other_gain(l) * cur, cur)
            leave_out[2 * l + 1] = cur
            cur = bwd_in[2 * l + 1, :ROWS] + gain_of(2 * l + 1) * cur
            leave_out[2 * l] = cur
            cur = bwd_in[2 * l, :ROWS] + gain_of(2 * l) * cur
            cur = jnp.where(is_left, cur, bwd_oth[l, :ROWS] + other_gain(l) * cur)
        send_back(leave_out, leave_in, plane, 4)

    @pl.when(early)
    def _():
        pl.semaphore_wait(ready, 3)
        tell_later(ready)

    for part in range(2):
        at = slice(part * HALF, part * HALF + HALF)
        left = is_left[at]
        cur = jnp.zeros((HALF, 128), jnp.float32)
        fwd_copies[part].wait_recv()
        for l in range(LINES):
            cur = jnp.where(left, cur, fwd_oth[part, l] + other_gain(l) * cur)
            enter_out[part, 2 * l] = cur
            cur = fwd_in[2 * l, at] + gain_of(2 * l) * cur
            enter_out[part, 2 * l + 1] = cur
            cur = fwd_in[2 * l + 1, at] + gain_of(2 * l + 1) * cur
            cur = jnp.where(left, fwd_oth[part, l] + other_gain(l) * cur, cur)
        send_all(enter_out.at[part], enter_in, at, 5)

    def core_exchange(n, part, at):
        copy = pltpu.make_async_remote_copy(
            src_ref=core_out.at[n, at, 1 - core], dst_ref=core_in.at[n, at], send_sem=core_sems.at[0, n, part],
            recv_sem=core_sems.at[1, n, part], device_id=other_core, device_id_type=MESH,
        )
        copy.start()
        return copy

    def send_part(n, to):
        slot = z_hi - (z_hi > to).astype(jnp.int32)
        pltpu.make_async_remote_copy(
            src_ref=part_out.at[n, to], dst_ref=part_in.at[n, slot],
            send_sem=part_send.at[n], recv_sem=part_recv.at[n],
            device_id={"head": to * 2 + core}, device_id_type=MESH,
        ).start()

    def sum_heads(n, local, scaled_ref, state_in):
        states = [
            state_in[block * 8 : block * 8 + 8].reshape(STATE, 128).astype(jnp.bfloat16)
            for block in range(BLOCKS)
        ]
        pieces = (slice(0, 1), slice(1, 4))
        exchanges = []
        for part, at in enumerate(pieces):
            rows = slice(at.start * 2 * PART, at.stop * 2 * PART)
            total = local[rows]
            for block in range(BLOCKS):
                total = total + dot(scaled_ref[rows, block * 128 : block * 128 + 128], states[block], NT)
            core_out[n, at] = total.reshape(at.stop - at.start, 2, PART, 128)
            exchanges.append(core_exchange(n, part, at))
        def settle(part):
            at = pieces[part]
            exchanges[part].wait_recv()
            part_out[n, at] = core_out[n, at, core] + core_in[n, at]

        settle(0)

        @pl.when(jnp.logical_not(early))
        def _():
            send_part(n, 0)

        later_sums.append(settle)
        copies.extend(exchanges)

    wait_bytes(leave_in, recv_sems.at[4])
    later_sums = []
    sum_heads(0, local_b, xs_ref, leave_in)
    wait_bytes(enter_in, recv_sems.at[5])
    sum_heads(1, local_c, ys_ref, enter_in)
    for block in range(BLOCKS):
        at = slice(block * 128, block * 128 + 128)
        leave = leave_in[block * 8 : block * 8 + 8].reshape(STATE, 128).astype(jnp.bfloat16)
        gx_ref[:, at] = (local_x[:, at] + end_ref[:, at] * dot(b_blk, leave, NN)).astype(jnp.bfloat16)
    stores = [pltpu.make_async_copy(gx_ref, gx_hbm, out_sems.at[0])]
    stores[0].start()
    for settle in later_sums:
        settle(1)

    @pl.when(jnp.logical_not(early))
    def _():
        pl.semaphore_wait(ready, 1)

    for n in range(2):
        for to in range(1, 4):
            @pl.when(z_hi != to)
            def _(n=n, to=to):
                send_part(n, to)

    wait_bytes(part_in.at[0], part_recv.at[0])

    for n, ref in ((1, bwd_in), (2, fwd_in), (4, leave_in), (5, enter_in)):
        wait_bytes(ref.at[pl.ds(0, GROUP - 1)], send_sems.at[n])
    for plane in range(4):
        at = slice(plane * 4, plane * 4 + 4)
        wait_bytes(bwd_tot.at[at], mid_bwd_sems.at[0, plane])
    for copy in fwd_copies:
        copy.wait_send()

    for n, (out, out_hbm) in enumerate(((gb_ref, gb_hbm), (gc_ref, gc_hbm))):
        if n == 1:
            wait_bytes(part_in.at[1], part_recv.at[1])
        out[...] = part_out[n, z_hi] + part_in[n, 0] + part_in[n, 1] + part_in[n, 2]
        stores.append(pltpu.make_async_copy(out, out_hbm, out_sems.at[1 + n]))
        stores[-1].start()
    for n in range(2):
        wait_bytes(part_in.at[n], part_send.at[n])
        for part in range(2):
            copies[2 * n + part].wait_send()
    for store in stores:
        store.wait()


def place(gx_in, gb_in, gc_in, gx_out, gb_out, gc_out, gx_buf, gb_buf, gc_buf, in_sems, out_sems):
    rows = Q // PIECES
    parts = [(gx_in.at[at], gx_buf.at[at], gx_out.at[at]) for at in (pl.ds(n * rows, rows) for n in range(PIECES))]
    parts += [(gb_in, gb_buf, gb_out), (gc_in, gc_buf, gc_out)]
    loads = [pltpu.make_async_copy(src, buf, in_sems.at[n]) for n, (src, buf, dst) in enumerate(parts)]
    stores = [pltpu.make_async_copy(buf, dst, out_sems.at[n]) for n, (src, buf, dst) in enumerate(parts)]
    for load in loads:
        load.start()
    for load, store in zip(loads, stores):
        load.wait()
        store.start()
    for store in stores:
        store.wait()


def on_device(x_seq, grad_out, b_proj, c_proj, decay_rate):
    def vmem(shape, dtype=jnp.float32):
        return pltpu.VMEM(shape, dtype)

    def dma(*shape):
        return pltpu.SemaphoreType.DMA(shape)

    chunks = (GROUP, ROWS, 128)
    totals = (2, LINES, HALF, 128)
    returns = (2, GROUP, HALF, 128)
    wide = (Q, HEADS * WIDTH)
    hbm = pl.BlockSpec(memory_space=pltpu.HBM)
    results = (
        jax.ShapeDtypeStruct(wide, jnp.bfloat16),
        jax.ShapeDtypeStruct((PART, STATE), jnp.float32),
        jax.ShapeDtypeStruct((PART, STATE), jnp.float32),
    )
    sums = pl.pallas_call(
        kernel,
        out_shape=results,
        in_specs=[hbm] * 5,
        out_specs=(hbm,) * 3,
        scratch_shapes=[
            vmem(wide, jnp.bfloat16), vmem(wide, jnp.bfloat16),
            vmem((Q, STATE), jnp.bfloat16), vmem((Q, STATE), jnp.bfloat16), vmem((HEADS, Q)),
            vmem(wide, jnp.bfloat16), vmem((PART, STATE)), vmem((PART, STATE)),
            vmem(chunks), vmem((GROUP, ROWS + 1, 128)), vmem(chunks), vmem((GROUP, ROWS + 1, 128)),
            vmem(totals), vmem((LINES, ROWS + 1, 128)), vmem(totals), vmem((LINES, ROWS + 1, 128)),
            vmem(returns), vmem(chunks), vmem(chunks), vmem(chunks),
            vmem(wide, jnp.bfloat16), vmem(wide, jnp.bfloat16),
            vmem(wide), vmem(wide),
            vmem((Q, STATE)), vmem((Q, STATE)),
            vmem((2, 4, 2, PART, 128)), vmem((2, 4, PART, 128)),
            vmem((2, 4, PART, 128)), vmem((2, 3, PART, 128)),
            dma(5), dma(6), dma(6), dma(4), dma(4), dma(2, 2), dma(2, 4),
            dma(2, 2, 2), dma(2), dma(2), dma(3), pltpu.SemaphoreType.REGULAR,
        ],
        compiler_params=pltpu.CompilerParams(
            collective_id=0, has_side_effects=True, vmem_limit_bytes=56 << 20
        ),
    )(x_seq, grad_out, b_proj, c_proj, decay_rate)
    return pl.pallas_call(
        place,
        out_shape=results,
        in_specs=[hbm] * 3,
        out_specs=(hbm,) * 3,
        scratch_shapes=[
            vmem(wide, jnp.bfloat16), vmem((PART, STATE)), vmem((PART, STATE)),
            dma(PIECES + 2), dma(PIECES + 2),
        ],
        compiler_params=pltpu.CompilerParams(vmem_limit_bytes=56 << 20),
    )(*sums)


def solution(mesh):
    placed = (P("ctx", "head"), P("ctx", "head"), P("ctx", None), P("ctx", None), P("head", "ctx"))
    return jax.shard_map(
        on_device,
        mesh=mesh,
        in_specs=placed,
        out_specs=(P("ctx", "head"), P(("ctx", "head"), None), P(("ctx", "head"), None)),
        check_vma=False,
    )
```
